128 devices in a mesh: ctx: 16 (over x, y), tp: 4 (over z), dp: 2 (over core).
Axes of the slice: x: 4, y: 4, z: 4, core: 2. Of those that a mesh axis runs over, the one named last changes fastest.
Arguments:
- grad_out: bfloat16 [2, 4096, 8192], P('dp', 'ctx'), may hold values from -6 to 6
- out_weight: bfloat16 [8192, 4096], P(None, 'tp'), may hold values from -0.09375 to 0.09375
- query_states: bfloat16 [2, 4096, 4096], P('dp', 'ctx', 'tp'), may hold values from -6 to 6
- key_states: bfloat16 [2, 4096, 512], P('dp', 'ctx', 'tp'), may hold values from -6 to 6
- value_tensor: bfloat16 [2, 4096, 512], P('dp', 'ctx', 'tp'), may hold values from -6 to 6
- attn_out: bfloat16 [2, 4096, 4096], P('dp', 'ctx', 'tp'), may hold values from -1.25 to 1.25
- doc_ids: int32 [2, 4096], P('dp'), may hold values from 0 to 31, never falling along the last dimension, each value on 1 to 1024 neighbouring positions
- block_order: int32 [2, 256], P('dp'), may hold values from 0 to 255, as said below
Outputs:
- query_grad: bfloat16 [2, 4096, 4096], P('dp', 'ctx', 'tp')
- key_gradient: bfloat16 [2, 4096, 512], P('dp', 'ctx', 'tp')
- value_gradient: bfloat16 [2, 4096, 512], P('dp', 'ctx', 'tp')
- weight_grad: float32 [8192, 4096], P(('ctx', 'dp'), 'tp')
The draws below stay inside these ranges and needn't reach their ends.
Inputs may be any that keep to these rules, and one draw needn't show every extreme that they name: `block_order`: for each micro-batch a permutation of the row blocks. The slots that one index of ctx holds in the owner layout receive at most 2 of the row blocks that any one index of ctx holds in token order, and in every draw some index hands exactly 2 blocks to one owner. `doc_ids`: document ids never fall along a micro-batch; every document has 1 to 1024 tokens and one has exactly 1024.
All inputs are finite; a program needn't handle non-finite values.
Results may differ from the reference program's by a relative error of at most 0.022.
Values may be sent and summed in bfloat16 or wider, within the bound.
No kernel may reach another device: no remote copies, remote signals or barrier semaphores. Data moves between devices by JAX's collectives and lax.ppermute only.
A program may use at most 128 MiB of HBM per device.

```python
import math
import jax
import jax.numpy as jnp
import numpy as np
from jax import lax

D = 8192
HQ = 32
KEY_VALUE_HEADS = 4
HEAD_WIDTH = 128
QUERY_PER_KEY = 8
TOK_DEV = 256
MICRO_BATCHES = 2
PACKED_TOKENS = 4096
BLOCK_ROWS = 16
BLOCKS = 256
DOCS = 32
DOC_MOST = 1024
N_CTX = 16


def draw_query_states(key, part):
    key = jax.random.fold_in(key, 17)
    tensor_dims = (MICRO_BATCHES, PACKED_TOKENS, KEY_VALUE_HEADS, QUERY_PER_KEY, HEAD_WIDTH)
    naive_result = jnp.clip(jax.random.normal(key, tensor_dims), -4.0, 4.0)
    return naive_result.reshape(MICRO_BATCHES, PACKED_TOKENS, HQ * HEAD_WIDTH).astype(jnp.bfloat16)


def draw_key_states(key, part):
    key = jax.random.fold_in(key, 29)
    tensor_dims = (MICRO_BATCHES, PACKED_TOKENS, KEY_VALUE_HEADS, HEAD_WIDTH)
    naive_result = jnp.clip(jax.random.normal(key, tensor_dims), -4.0, 4.0)
    return naive_result.reshape(MICRO_BATCHES, PACKED_TOKENS, KEY_VALUE_HEADS * HEAD_WIDTH).astype(jnp.bfloat16)


def draw_block_order(key, part):
    key = jax.random.fold_in(key, 41)
    devices = PACKED_TOKENS // TOK_DEV

    def draw_batch(batch_key):
        rank_key, shift_key, twin_key, place_key = jax.random.split(batch_key, 4)
        spread = jax.random.permutation(rank_key, devices)
        shifts = jax.random.permutation(shift_key, devices)
        twin_round = jax.random.randint(twin_key, (), 1, devices)
        shifts = shifts.at[twin_round].set(shifts[0])
        places = jax.vmap(lambda place_sub: jax.random.permutation(place_sub, devices))(jax.random.split(place_key, devices))
        source = jnp.arange(devices)[:, None]
        rounds = jnp.arange(devices)[None, :]
        owner = spread[(source + shifts[None, :]) % devices]
        slot_index = owner * devices + places[owner, rounds]
        block_index = source * devices + rounds
        return jnp.zeros(devices * devices, jnp.int32).at[slot_index.reshape(-1)].set(block_index.reshape(-1).astype(jnp.int32))
    return jax.vmap(draw_batch)(jax.random.split(key, MICRO_BATCHES))


def raised(entries, stream_key, source, target, parts, factor):
    def block_of(axis_at):
        return (jnp.arange(entries.shape[axis_at]) // (entries.shape[axis_at] // parts)).reshape((-1,) + (1,) * (entries.ndim - 1 - axis_at))

    near = jax.random.permutation(stream_key, parts)[block_of(target)]
    other_side = (block_of(target) + parts // 2) % parts
    return jnp.where((block_of(source) == near) | (block_of(source) == other_side), factor * entries, entries)


def level_of(own_key, extent, cuts, least, largest):
    gain, own = 1.0, jax.random.fold_in(own_key, 6)
    for axis_at, shards_of in cuts:
        heights = jnp.exp(jax.random.uniform(jax.random.fold_in(own, axis_at), (shards_of,), jnp.float32, least / len(cuts), largest / len(cuts)))
        gain = gain * jnp.repeat(heights, extent[axis_at] // shards_of).reshape([-1 if axis == axis_at else 1 for axis in range(len(extent))])
    return gain


def split_up(number_of, total, limit, lean):
    loads = [(1 << 20) // math.isqrt(grade ** lean) + 1 for grade in range(2, number_of + 1)]
    spare, counts = total - limit - (number_of - 1), [1] * (number_of - 1)
    while spare > 0:
        movable = [i for i in range(number_of - 1) if counts[i] < limit]
        whole, remaining = sum([loads[i] for i in movable]), spare
        for i in movable:
            addition = min(limit - counts[i], max(1, remaining * loads[i] // whole), spare)
            counts[i] = counts[i] + addition
            spare = spare - addition
    return np.array([limit] + counts)


def uneven(rng, number_of, total, bound, skew):
    if number_of == 2:
        one = jax.random.randint(rng, (), max(1, total - bound), min(bound, total - 1) + 1)
        return jnp.stack([one, total - one])
    sizes = jnp.asarray(split_up(number_of, total, bound, skew), jnp.int32)
    couples = (number_of - 1) // 2
    giver, sink = sizes[1:1 + 2 * couples:2], sizes[2:2 + 2 * couples:2]
    slack = jnp.minimum(giver - 1, bound - sink)
    shifted = jax.random.randint(jax.random.fold_in(rng, 1), (couples,), 0, 1 << 20) % (slack + 1)
    sizes = sizes.at[1:1 + 2 * couples:2].set(giver - shifted).at[2:2 + 2 * couples:2].set(sink + shifted)
    return sizes[jax.random.permutation(jax.random.fold_in(rng, 2), number_of)]


def noise(own_key, shape, scale, bound, shards=(), held_as=jnp.bfloat16):
    result = jax.random.normal(own_key, shape, jnp.float32) * scale
    if len(shards) > 0:
        result = level_of(own_key, shape, shards, -0.22, 0.18) * result
    return jnp.clip(result, min=-bound, max=bound).astype(held_as)


def noise_with(rng, shape, width, limit, pieces, heavy, kind=jnp.bfloat16):
    values = width * jax.random.normal(rng, shape, jnp.float32)
    if pieces:
        values = values * level_of(rng, shape, pieces, -0.22, 0.18)
    return jnp.clip(raised(values, jax.random.fold_in(rng, 3), *heavy), -limit, limit).astype(kind)


def setup_inputs(seed: int = 0) -> dict:
    key_of = jax.random.split(jax.random.key(seed), 9)
    grad_out = noise_with(key_of[0], (MICRO_BATCHES, PACKED_TOKENS, D), 1.0, 6.0, ((0, 2), (1, 16)), (1, 2, 16, 2.0))
    out_weight = noise(key_of[1], (D, HQ * HEAD_WIDTH), (HQ * HEAD_WIDTH) ** -0.5, 0.09375, ((1, 4),))
    query_states = draw_query_states(jax.random.fold_in(key_of[8], 71), 0)
    key_states = draw_key_states(jax.random.fold_in(key_of[8], 71), 0)
    value_tensor = noise(key_of[4], (MICRO_BATCHES, PACKED_TOKENS, KEY_VALUE_HEADS * HEAD_WIDTH), 1.0, 6.0, ((0, 2), (1, 16), (2, 4)))
    attn_out = noise(key_of[5], (MICRO_BATCHES, PACKED_TOKENS, HQ * HEAD_WIDTH), 0.2, 1.25, ((0, 2), (1, 16), (2, 4)))
    doc_ids = jax.vmap(lambda own: jnp.searchsorted(jnp.cumsum(uneven(own, DOCS, PACKED_TOKENS, DOC_MOST, 2)), jnp.arange(PACKED_TOKENS), side="right"))(jax.random.split(key_of[6], MICRO_BATCHES)).reshape((MICRO_BATCHES, PACKED_TOKENS)).astype(jnp.int32)
    block_order = draw_block_order(jax.random.fold_in(key_of[8], 71), 0)
    return {"grad_out": grad_out, "out_weight": out_weight, "query_states": query_states, "key_states": key_states, "value_tensor": value_tensor, "attn_out": attn_out, "doc_ids": doc_ids, "block_order": block_order}


def head_grads(operands, doc_row):
    query_head, grad_head, out_head, key_head, value_head = operands
    score_scale = 1.0 / math.sqrt(HEAD_WIDTH)
    positions = jnp.arange(PACKED_TOKENS, dtype=jnp.int32)
    allowed = (doc_row[:, None] == doc_row[None, :]) & (positions[None, :] <= positions[:, None])
    scores = jnp.dot(query_head, key_head.T, preferred_element_type=jnp.float32) * score_scale
    row_max = lax.optimization_barrier(jnp.max(jnp.where(allowed, scores, -jnp.inf), axis=1))
    row_sum = lax.optimization_barrier(jnp.sum(jnp.exp(jnp.where(allowed, scores - row_max[:, None], -jnp.inf)), axis=1))
    log_norm = row_max + jnp.log(row_sum)
    attn_probs = jnp.exp(jnp.where(allowed, scores - log_norm[:, None], -jnp.inf))
    probs_low = attn_probs.astype(jnp.bfloat16)
    value_fragment = jnp.dot(probs_low.T, grad_head, preferred_element_type=jnp.float32)
    prob_grad = jnp.dot(grad_head, value_head.T, preferred_element_type=jnp.float32)
    row_dot = lax.optimization_barrier(jnp.sum(grad_head.astype(jnp.float32) * out_head.astype(jnp.float32), axis=1))
    score_grad = (attn_probs * (prob_grad - row_dot[:, None])).astype(jnp.bfloat16)
    query_part = jnp.dot(score_grad, key_head, preferred_element_type=jnp.float32) * score_scale
    key_fragment = jnp.dot(score_grad.T, query_head, preferred_element_type=jnp.float32) * score_scale
    return (query_part, key_fragment, value_fragment)

def separate_heads(matrix, heads):
    return jnp.transpose(matrix.reshape(PACKED_TOKENS, heads, HEAD_WIDTH), (1, 0, 2))

def merge_heads(stacked, heads):
    return jnp.transpose(stacked, (1, 0, 2)).reshape(PACKED_TOKENS, heads * HEAD_WIDTH)

def batch_grads(grad_rows, query_rows, key_row_block, value_row_block, out_rows, doc_row, slot_blocks, out_weight):
    attn_grad = jnp.dot(grad_rows, out_weight, preferred_element_type=jnp.float32).astype(jnp.bfloat16)
    keys_repeated = jnp.repeat(separate_heads(key_row_block, KEY_VALUE_HEADS), QUERY_PER_KEY, axis=0)
    values_repeated = jnp.repeat(separate_heads(value_row_block, KEY_VALUE_HEADS), QUERY_PER_KEY, axis=0)
    operands = (separate_heads(query_rows, HQ), separate_heads(attn_grad, HQ), separate_heads(out_rows, HQ), keys_repeated, values_repeated)
    query_part, key_fragment, value_fragment = lax.map(lambda item: head_grads(item, doc_row), operands)
    full_query = merge_heads(query_part, HQ).astype(jnp.bfloat16)
    key_gradient = merge_heads(lax.optimization_barrier(jnp.sum(key_fragment.reshape(KEY_VALUE_HEADS, QUERY_PER_KEY, PACKED_TOKENS, HEAD_WIDTH), axis=1)), KEY_VALUE_HEADS).astype(jnp.bfloat16)
    value_gradient = merge_heads(lax.optimization_barrier(jnp.sum(value_fragment.reshape(KEY_VALUE_HEADS, QUERY_PER_KEY, PACKED_TOKENS, HEAD_WIDTH), axis=1)), KEY_VALUE_HEADS).astype(jnp.bfloat16)
    blocked = full_query.reshape(BLOCKS, BLOCK_ROWS, HQ * HEAD_WIDTH)
    owned = jnp.take(blocked, slot_blocks.astype(jnp.int32), axis=0).reshape(PACKED_TOKENS, HQ * HEAD_WIDTH)
    return (owned, key_gradient, value_gradient)

def reference(grad_out, out_weight, query_states, key_states, value_tensor, attn_out, doc_ids, block_order):
    results = [batch_grads(grad_out[batch_index], query_states[batch_index], key_states[batch_index], value_tensor[batch_index], attn_out[batch_index], doc_ids[batch_index], block_order[batch_index], out_weight) for batch_index in range(MICRO_BATCHES)]
    query_grad = jnp.stack([item[0] for item in results])
    key_gradient = jnp.stack([item[1] for item in results])
    value_gradient = jnp.stack([item[2] for item in results])

    def add_partial(running, flat_index):
        batch_index = (flat_index // N_CTX).astype(jnp.int32)
        offset = (flat_index % N_CTX * TOK_DEV).astype(jnp.int32)
        zero_index = (flat_index * 0).astype(jnp.int32)
        grad_rows = lax.dynamic_slice(grad_out, (batch_index, offset, zero_index), (1, TOK_DEV, D))[0]
        out_rows = lax.dynamic_slice(attn_out, (batch_index, offset, zero_index), (1, TOK_DEV, HQ * HEAD_WIDTH))[0]
        partial_value = lax.dot_general(grad_rows, out_rows, (((0,), (0,)), ((), ())), preferred_element_type=jnp.float32).astype(jnp.bfloat16)
        return (running + lax.optimization_barrier(partial_value).astype(jnp.float32), None)
    weight_grad, leftover = lax.scan(add_partial, jnp.zeros((D, HQ * HEAD_WIDTH), jnp.float32), jnp.arange(MICRO_BATCHES * N_CTX, dtype=jnp.int32))
    return (query_grad, key_gradient, value_gradient, weight_grad)
```

```python
import math

import jax
import jax.numpy as jnp
from jax import lax
from jax.experimental import pallas as pl
from jax.experimental.pallas import tpu as pltpu
from jax.sharding import PartitionSpec as P

HEAD = 128
CAP = 2
SIDE = 4
BACK = 4
RUN = 256
BLK = 256
COLS = 256
NEG = -1e30
MIB = 1024 * 1024
NT = (((1,), (1,)), ((), ()))
TN = (((0,), (0,)), ((), ()))


def grid_shift(dx, dy):
    return [
        (x * SIDE + y, ((x + dx) % SIDE) * SIDE + (y + dy) % SIDE)
        for x in range(SIDE)
        for y in range(SIDE)
    ]


def run_shift(k, parties):
    return [(i, (i + k) % parties) for i in range(parties)]


XP, XM, YP, YM = (1, 0), (-1, 0), (0, 1), (0, -1)


def hop(value, way):
    return lax.ppermute(value, "ctx", grid_shift(*way))


def swap_cores(value):
    return lax.ppermute(value, "dp", [(0, 1), (1, 0)])


def pick_kernel(core_ref, in_ref, out_ref):
    out_ref[...] = in_ref[...]


def other_half(grad_rows, core):
    tokens, width = grad_rows.shape
    return pl.pallas_call(
        pick_kernel,
        grid_spec=pltpu.PrefetchScalarGridSpec(
            num_scalar_prefetch=1,
            grid=(width // (2 * BLK),),
            in_specs=[pl.BlockSpec((tokens, BLK), lambda i, core_ref: (0, 2 * i + 1 - core_ref[0]))],
            out_specs=pl.BlockSpec((tokens, BLK), lambda i, core_ref: (0, i)),
        ),
        out_shape=jax.ShapeDtypeStruct((tokens, width // 2), grad_rows.dtype),
        cost_estimate=pl.CostEstimate(
            flops=0, bytes_accessed=2 * tokens * width, transcendentals=0
        ),
        name="other_half",
    )(core.reshape(1), grad_rows)


def pieces(table, core, grads, outs, specs, steps, dtype, joined=False, name="pieces"):
    grad_own, grad_rec = grads
    out_own, out_rec = outs
    tokens = out_own.shape[0]
    flat = jnp.concatenate([jnp.stack([jnp.int32(0) + v for v in row]) for row in table])
    flat = jnp.concatenate([flat, core.reshape(1)]).astype(jnp.int32)
    core_at = len(table) * steps
    in_specs, operands = [], []
    for row, _, _ in specs:
        in_specs.append(
            pl.BlockSpec((tokens, BLK), lambda j, t, row=row: (0, 2 * t[row * steps + j] + t[core_at]))
        )
        operands.append(grad_own)
        in_specs.append(pl.BlockSpec((tokens, BLK), lambda j, t, row=row: (0, t[row * steps + j])))
        operands.append(grad_rec)
    for value in (out_own, out_rec):
        in_specs.append(pl.BlockSpec(value.shape, lambda j, t: (0, 0)))
        operands.append(value)
    for _, _, arrived in specs:
        for value, row in arrived:
            in_specs.append(
                pl.BlockSpec((BLK, COLS), lambda j, t, row=row: (t[row * steps + j], 0))
            )
            operands.append(value)
    count = len(specs)

    def kernel(table_ref, *refs):
        ins, results = refs[: len(operands)], refs[len(operands) :]
        own_ref, rec_ref = ins[2 * count], ins[2 * count + 1]
        at = 2 * count + 2
        for n, (_, col, arrived) in enumerate(specs):
            total = lax.dot_general(
                ins[2 * n][...],
                own_ref[:, col : col + COLS],
                TN,
                preferred_element_type=jnp.float32,
            )
            total = total + lax.dot_general(
                ins[2 * n + 1][...],
                rec_ref[:, col : col + COLS],
                TN,
                preferred_element_type=jnp.float32,
            )
            for _ in arrived:
                total = total + ins[at][...].astype(jnp.float32)
                at += 1
            if joined:
                results[0][:, col : col + COLS] = total.astype(dtype)
            else:
                results[n][...] = total.astype(dtype)

    if joined:
        out_specs = [pl.BlockSpec((BLK, count * COLS), lambda j, t: (j, 0))]
        out_shape = [jax.ShapeDtypeStruct((steps * BLK, count * COLS), dtype)]
    else:
        out_specs = [pl.BlockSpec((BLK, COLS), lambda j, t: (j, 0))] * count
        out_shape = [jax.ShapeDtypeStruct((steps * BLK, COLS), dtype)] * count
    return pl.pallas_call(
        kernel,
        grid_spec=pltpu.PrefetchScalarGridSpec(
            num_scalar_prefetch=1, grid=(steps,), in_specs=in_specs, out_specs=out_specs
        ),
        out_shape=out_shape,
        compiler_params=pltpu.CompilerParams(vmem_limit_bytes=32 * MIB),
        cost_estimate=pl.CostEstimate(
            flops=4 * count * steps * tokens * BLK * COLS,
            bytes_accessed=count * steps * (4 * tokens * BLK + 4 * BLK * COLS) + 4 * out_own.size,
            transcendentals=0,
        ),
        name=name,
    )(flat, *operands)


def weight_gradient(grad_rows, out_rows, x, y, core):
    grads = (grad_rows, swap_cores(other_half(grad_rows, core)))
    outs = (out_rows, swap_cores(out_rows))
    four = range(SIDE)
    xa, xb, ya, yb = 0, COLS, 2 * COLS, 3 * COLS

    def along(dx):
        return [((x + dx) % SIDE) * SIDE + j for j in four]

    def across(dy):
        return [j * SIDE + (y + dy) % SIDE for j in four]

    def make(name, table, specs, steps):
        return pieces(table, core, grads, outs, specs, steps, jnp.bfloat16, name=name)

    far = make(
        "far",
        [along(2), across(2)],
        [(0, xa, []), (0, xb, []), (1, ya, []), (1, yb, [])],
        SIDE,
    )
    far = [hop(v, w) for v, w in zip(far, (XP, XM, YP, YM))]
    sides = [along(1), along(-1), across(1), across(-1)]
    near = make("near", sides, [(0, xb, []), (1, xa, []), (2, yb, []), (3, ya, [])], SIDE)
    near = [hop(v, w) for v, w in zip(near, (XP, XM, YP, YM))]
    both = make(
        "both",
        sides + [list(four)],
        [
            (0, xa, [(far[0], 4)]),
            (1, xb, [(far[1], 4)]),
            (2, ya, [(far[2], 4)]),
            (3, yb, [(far[3], 4)]),
        ],
        SIDE,
    )
    both = [hop(v, w) for v, w in zip(both, (XP, XM, YP, YM))]
    got_xa = lambda row: [(both[0], row), (near[1], row)]
    got_xb = lambda row: [(near[0], row), (both[1], row)]
    got_ya = lambda row: [(both[2], row), (near[3], row)]
    got_yb = lambda row: [(near[2], row), (both[3], row)]

    def block(dx, dy):
        return ((x + dx) % SIDE) * SIDE + (y + dy) % SIDE

    y2, y1, y3 = (y + 2) % SIDE, (y + 1) % SIDE, (y + 3) % SIDE
    x2, x1, x3 = (x + 2) % SIDE, (x + 1) % SIDE, (x + 3) % SIDE
    sends = make(
        "sends",
        [[v] for v in (block(0, 2), block(2, 0), block(0, 1), block(0, 3), block(1, 0), block(3, 0))]
        + [[v] for v in (y2, x2, y1, y3, x1, x3)],
        [
            (0, xa, got_xa(6)),
            (0, xb, got_xb(6)),
            (1, ya, got_ya(7)),
            (1, yb, got_yb(7)),
            (2, xb, got_xb(8)),
            (3, xa, got_xa(9)),
            (4, yb, got_yb(10)),
            (5, ya, got_ya(11)),
        ],
        1,
    )
    sends = [hop(v, w) for v, w in zip(sends, (YP, YM, XP, XM) * 2)]
    last = make(
        "last",
        [[v] for v in (block(0, 1), block(0, 3), block(1, 0), block(3, 0), y1, y3, x1, x3)] + [[0]],
        [
            (0, xa, got_xa(4) + [(sends[0], 8)]),
            (1, xb, got_xb(5) + [(sends[1], 8)]),
            (2, ya, got_ya(6) + [(sends[2], 8)]),
            (3, yb, got_yb(7) + [(sends[3], 8)]),
        ],
        1,
    )
    last = [hop(v, w) for v, w in zip(last, (YP, YM, XP, XM))]
    return pieces(
        [[block(0, 0)], [y], [x], [0]],
        core,
        grads,
        outs,
        [
            (0, xa, got_xa(1) + [(last[0], 3), (sends[5], 3)]),
            (0, xb, got_xb(1) + [(last[1], 3), (sends[4], 3)]),
            (0, ya, got_ya(2) + [(last[2], 3), (sends[7], 3)]),
            (0, yb, got_yb(2) + [(last[3], 3), (sends[6], 3)]),
        ],
        1,
        jnp.float32,
        joined=True,
        name="total",
    )[0]


def attend_kernel(
    low_ref, pos_ref, q_ref, g_ref, o_ref, key_ref, val_ref,
    kv4, kv3, kv2, kv1,
    packed_ref, own_ref, back4, back3, back2, back1,
    bias, keys, keys_t, vals, dkey, dval,
):
    head = pl.program_id(0)
    scale = 1.0 / math.sqrt(HEAD)
    window = bias.shape[0]

    @pl.when(head == 0)
    def _():
        row = lax.broadcasted_iota(jnp.int32, bias.shape, 0)
        col = lax.broadcasted_iota(jnp.int32, bias.shape, 1)
        seen = (row >= low_ref[...]) & (row <= col + BACK * RUN)
        bias[...] = jnp.where(seen, 0.0, NEG)
        for n, ref in enumerate((kv4, kv3, kv2, kv1)):
            keys[n * RUN : (n + 1) * RUN, :] = ref[:, :HEAD]
            vals[n * RUN : (n + 1) * RUN, :] = ref[:, HEAD:]
        keys[BACK * RUN :, :] = key_ref[...]
        vals[BACK * RUN :, :] = val_ref[...]
        keys_t[...] = keys[...].T
        dkey[...] = jnp.zeros_like(dkey)
        dval[...] = jnp.zeros_like(dval)

    q = q_ref[...]
    g = g_ref[...]
    prod = g.astype(jnp.float32) * o_ref[...].astype(jnp.float32)
    row_dot = jnp.sum(prod.T, axis=0, keepdims=True)
    scores = lax.dot_general(keys[...], q, NT, preferred_element_type=jnp.float32)
    scores = scores * (scale * math.log2(math.e)) + bias[...]
    top = jnp.max(scores, axis=0, keepdims=True)
    probs = jnp.exp2(scores - top)
    probs = probs * (1.0 / jnp.sum(probs, axis=0, keepdims=True))
    dval[...] += jnp.dot(probs.astype(jnp.bfloat16), g, preferred_element_type=jnp.float32)
    prob_grad = lax.dot_general(vals[...], g, NT, preferred_element_type=jnp.float32)
    score_grad = (probs * (prob_grad - row_dot)).astype(jnp.bfloat16)
    dkey[...] += jnp.dot(score_grad, q, preferred_element_type=jnp.float32)
    dq_t = jnp.dot(keys_t[...], score_grad, preferred_element_type=jnp.float32) * scale
    dq = dq_t.T.astype(jnp.bfloat16)
    slots = lax.broadcasted_iota(jnp.int32, (packed_ref.shape[0], RUN), 0)
    select = (slots == pos_ref[...]).astype(jnp.bfloat16)
    packed_ref[...] = jnp.dot(select, dq, preferred_element_type=jnp.float32).astype(jnp.bfloat16)

    @pl.when(head == pl.num_programs(0) - 1)
    def _():
        for n, ref in enumerate((back4, back3, back2, back1)):
            rows = slice(n * RUN, (n + 1) * RUN)
            ref[:, :HEAD] = (dkey[rows, :] * scale).astype(jnp.bfloat16)
            ref[:, HEAD:] = dval[rows, :].astype(jnp.bfloat16)
        own_ref[:, :HEAD] = dkey[BACK * RUN :, :] * scale
        own_ref[:, HEAD:] = dval[BACK * RUN :, :]


def attend(low, pos, query, grad, out, key, value, earlier, slots):
    heads = query.shape[1] // HEAD
    window = (BACK + 1) * RUN
    whole = lambda shape: pl.BlockSpec(shape, lambda h: (0, 0))
    by_head = lambda rows: pl.BlockSpec((rows, HEAD), lambda h: (0, h))
    pair = (RUN, 2 * HEAD)
    return pl.pallas_call(
        attend_kernel,
        grid=(heads,),
        in_specs=[whole((1, RUN))] * 2
        + [by_head(RUN)] * 3
        + [whole((RUN, HEAD))] * 2
        + [whole(pair)] * BACK,
        out_specs=[by_head(slots), whole(pair)] + [whole(pair)] * BACK,
        out_shape=[
            jax.ShapeDtypeStruct((slots, query.shape[1]), jnp.bfloat16),
            jax.ShapeDtypeStruct(pair, jnp.float32),
        ]
        + [jax.ShapeDtypeStruct(pair, jnp.bfloat16)] * BACK,
        scratch_shapes=[
            pltpu.VMEM((window, RUN), jnp.float32),
            pltpu.VMEM((window, HEAD), jnp.bfloat16),
            pltpu.VMEM((HEAD, window), jnp.bfloat16),
            pltpu.VMEM((window, HEAD), jnp.bfloat16),
            pltpu.VMEM((window, HEAD), jnp.float32),
            pltpu.VMEM((window, HEAD), jnp.float32),
        ],
        compiler_params=pltpu.CompilerParams(vmem_limit_bytes=40 * MIB),
        cost_estimate=pl.CostEstimate(
            flops=10 * heads * RUN * window * HEAD,
            bytes_accessed=8 * MIB,
            transcendentals=heads * RUN * window,
        ),
        name="attend",
    )(low, pos, query, grad, out, key, value, *earlier)


def route_rows(slot_blocks, own_index, parties, block_rows):
    total = slot_blocks.shape[0]
    ids = jnp.arange(total, dtype=jnp.int32)
    slot_of_block = jnp.sum(
        jnp.where(slot_blocks[None, :] == ids[:, None], ids[None, :], 0), axis=1
    )
    local = jnp.arange(parties, dtype=jnp.int32)

    def place(peer, order):
        earlier = (peer[:, None] == peer[None, :]) & (order[None, :] < order[:, None])
        return peer * CAP + jnp.sum(earlier, axis=1).astype(jnp.int32)

    dest_slot = lax.dynamic_slice_in_dim(slot_of_block, own_index * parties, parties, 0)
    held = lax.dynamic_slice_in_dim(slot_blocks, own_index * parties, parties, 0)
    rows = jnp.arange(block_rows, dtype=jnp.int32)

    def spread(at):
        return (at[:, None] * block_rows + rows[None, :]).reshape(-1)

    return spread(place(dest_slot // parties, dest_slot)), spread(place(held // parties, local))


def on_device(
    grad_out, out_weight, query_states, key_states, value_tensor, attn_out, doc_ids, block_order
):
    parties = lax.axis_size("ctx")
    own_index = lax.axis_index("ctx")
    core = lax.axis_index("dp")
    x, y = own_index // SIDE, own_index % SIDE
    grad_rows, out_rows = grad_out[0], attn_out[0]
    doc_row = doc_ids[0]
    key, value = key_states[0], value_tensor[0]

    both = jnp.concatenate([key, value], axis=1)
    earlier = [lax.ppermute(both, "ctx", run_shift(k, parties)) for k in range(BACK, 0, -1)]

    weight_grad = weight_gradient(grad_rows, out_rows, x, y, core)

    attn_grad = jnp.dot(grad_rows, out_weight, preferred_element_type=jnp.float32).astype(
        jnp.bfloat16
    )
    own_docs = lax.dynamic_slice_in_dim(doc_row, own_index * RUN, RUN, 0)
    first = jnp.sum((doc_row[:, None] < own_docs[None, :]).astype(jnp.int32), axis=0)
    low = (first - (own_index - BACK) * RUN).reshape(1, RUN)
    send_rows, held_rows = route_rows(block_order[0], own_index, parties, RUN // parties)
    slots = CAP * RUN
    packed, own_kv, *back = attend(
        low,
        send_rows.reshape(1, RUN),
        query_states[0],
        attn_grad,
        out_rows,
        key,
        value,
        earlier,
        slots,
    )
    got = lax.all_to_all(
        packed.reshape(parties, slots // parties, -1), "ctx", 0, 0, tiled=True
    ).reshape(slots, -1)
    held_select = (
        held_rows[:, None] == jnp.arange(slots, dtype=jnp.int32)[None, :]
    ).astype(jnp.bfloat16)
    query_grad = jnp.dot(held_select, got, preferred_element_type=jnp.float32).astype(jnp.bfloat16)
    returned = [
        lax.ppermute(v, "ctx", run_shift(-k, parties)) for v, k in zip(back, range(BACK, 0, -1))
    ]
    kv_sum = own_kv
    for v in returned:
        kv_sum = kv_sum + v.astype(jnp.float32)
    kv_sum = kv_sum.astype(jnp.bfloat16)
    return (
        query_grad[None],
        kv_sum[None, :, :HEAD],
        kv_sum[None, :, HEAD:],
        weight_grad,
    )


def solution(mesh):
    heads = P("dp", "ctx", "tp")
    in_specs = (
        P("dp", "ctx", None),
        P(None, "tp"),
        heads,
        heads,
        heads,
        heads,
        P("dp", None),
        P("dp", None),
    )
    out_specs = (heads, heads, heads, P(("ctx", "dp"), "tp"))
    return jax.shard_map(
        on_device, mesh=mesh, in_specs=in_specs, out_specs=out_specs, check_vma=False
    )
```

```python
import math

import jax
import jax.numpy as jnp
from jax import lax
from jax.experimental import pallas as pl
from jax.experimental.pallas import tpu as pltpu
from jax.sharding import PartitionSpec as P

HEAD = 128
CAP = 2
SIDE = 4
BACK = 4
RUN = 256
BLK = 256
TILE = 128
SEEN = BACK * RUN + TILE
CHUNK = 384
STACK = 2
VMEM = 56 * 1024 * 1024
WIDE = 512
NEG = -1e30
MIB = 1024 * 1024
NT = (((1,), (1,)), ((), ()))
TN = (((0,), (0,)), ((), ()))


def run_shift(k, parties):
    return [(i, (i + k) % parties) for i in range(parties)]


def axis_shift(k, second):
    pairs = []
    for x in range(SIDE):
        for y in range(SIDE):
            for core in range(2):
                along_x = (core == 0) != second
                to_x, to_y = ((x + k) % SIDE, y) if along_x else (x, (y + k) % SIDE)
                pairs.append(((x * SIDE + y) * 2 + core, (to_x * SIDE + to_y) * 2 + core))
    return pairs


def hop(value, k, second=False):
    return lax.ppermute(value, ("ctx", "dp"), axis_shift(k, second))


def swap_cores(value):
    return lax.ppermute(value, "dp", [(0, 1), (1, 0)])


def params():
    return pltpu.CompilerParams(vmem_limit_bytes=VMEM)


def cost(flops, moved, exps=0):
    return pl.CostEstimate(flops=flops, bytes_accessed=moved, transcendentals=exps)


def pick_kernel(core_ref, in_ref, out_ref, sems):
    other = 1 - core_ref[0]
    copies = []
    for i in range(out_ref.shape[1] // BLK):
        start = pl.multiple_of((2 * i + other) * BLK, BLK)
        copies.append(
            pltpu.make_async_copy(
                in_ref.at[:, pl.ds(start, BLK)], out_ref.at[:, i * BLK : (i + 1) * BLK], sems.at[i]
            )
        )
    for copy in copies:
        copy.start()
    for copy in copies:
        copy.wait()


def other_half(grad_rows, core):
    tokens, width = grad_rows.shape
    return pl.pallas_call(
        pick_kernel,
        in_specs=[pl.BlockSpec(memory_space=pltpu.SMEM), pl.BlockSpec(memory_space=pl.ANY)],
        out_specs=pl.BlockSpec(memory_space=pltpu.VMEM),
        out_shape=jax.ShapeDtypeStruct((tokens, width // 2), grad_rows.dtype),
        scratch_shapes=[pltpu.SemaphoreType.DMA((width // (2 * BLK),))],
        compiler_params=params(),
        cost_estimate=cost(0, 2 * tokens * width),
        name="other_half",
    )(core.reshape(1), grad_rows)


def project_kernel(grad_ref, weight_ref, out_ref, grads, weights, grad_sems, weight_sems):
    slabs = grad_sems.shape[0]
    depth = weight_ref.shape[0] // slabs
    copies = []
    for i in range(slabs):
        part = slice(i * depth, (i + 1) * depth)
        copies.append(
            (
                pltpu.make_async_copy(grad_ref.at[:, part], grads.at[:, part], grad_sems.at[i]),
                pltpu.make_async_copy(weight_ref.at[part], weights.at[part], weight_sems.at[i]),
            )
        )
    for pair in copies:
        for copy in pair:
            copy.start()
    total = None
    for i, pair in enumerate(copies):
        for copy in pair:
            copy.wait()
        part = slice(i * depth, (i + 1) * depth)
        addend = jnp.dot(grads[:, part], weights[part, :], preferred_element_type=jnp.float32)
        total = addend if total is None else total + addend
    out_ref[...] = total.astype(out_ref.dtype)


def project(grad_rows, weight):
    rows, depth = grad_rows.shape
    cols = weight.shape[1]
    slabs = 8
    return pl.pallas_call(
        project_kernel,
        in_specs=[pl.BlockSpec(memory_space=pl.ANY)] * 2,
        out_specs=pl.BlockSpec(memory_space=pltpu.VMEM),
        out_shape=jax.ShapeDtypeStruct((rows, cols), jnp.bfloat16),
        scratch_shapes=[
            pltpu.VMEM(grad_rows.shape, grad_rows.dtype),
            pltpu.VMEM(weight.shape, weight.dtype),
            pltpu.SemaphoreType.DMA((slabs,)),
            pltpu.SemaphoreType.DMA((slabs,)),
        ],
        compiler_params=params(),
        cost_estimate=cost(2 * rows * depth * cols, 2 * depth * (rows + cols)),
        name="project",
    )(grad_rows, weight)


def block_table(x, y, core):
    first, second = jnp.where(core == 0, x, y), jnp.where(core == 0, y, x)
    step_first, step_second = jnp.where(core == 0, SIDE, 1), jnp.where(core == 0, 1, SIDE)
    offsets = jnp.arange(SIDE, dtype=jnp.int32)
    blocks = ((first + offsets[:, None]) % SIDE) * step_first + offsets[None, :] * step_second
    order = (second + jnp.array([2, 1, 3, 0], jnp.int32)) % SIDE
    table = jnp.concatenate([blocks.reshape(-1), order, core.reshape(1)])
    return table.astype(jnp.int32)


ORDER, CORE = SIDE * SIDE, SIDE * SIDE + SIDE


def piece_kernel(plan, arrived_count, out_count, blocks, *refs):
    grad_own, grad_rec, out_own, out_rec = refs[:4]
    arrived_refs = refs[4 : 4 + arrived_count]
    refs = refs[-(out_count + 6) :] if arrived_count else refs[-(out_count + 5) :]
    results = refs[:out_count]
    if arrived_count:
        outs, grads, held, sent, in_sems, out_sems = refs[out_count:]
    else:
        outs, grads, sent, in_sems, out_sems = refs[out_count:]
    tokens = out_own.shape[0]
    core = blocks[CORE]
    taken = 0

    def load(source, target):
        nonlocal taken
        copy = pltpu.make_async_copy(source, target, in_sems.at[taken])
        taken += 1
        copy.start()
        return copy

    shared = [load(out_own, outs.at[:tokens]), load(out_rec, outs.at[tokens:])]
    loads, slot = [], 0
    for n, (at, parts) in enumerate(plan):
        block = blocks[at] if isinstance(at, int) else blocks[blocks[at[0]]]
        own = pl.multiple_of((2 * block + core) * BLK, BLK)
        rec = pl.multiple_of(block * BLK, BLK)
        copies = [
            load(grad_own.at[:, pl.ds(own, BLK)], grads.at[n, :tokens]),
            load(grad_rec.at[:, pl.ds(rec, BLK)], grads.at[n, tokens:]),
        ]
        slots = []
        for _, arrived, _, _, _ in parts:
            mine = []
            for which, row, col in arrived:
                first = row if isinstance(row, int) else blocks[row[0]]
                source = arrived_refs[which].at[
                    pl.ds(pl.multiple_of(first * BLK, BLK), BLK), col : col + WIDE
                ]
                copies.append(load(source, held.at[slot]))
                mine.append(slot)
                slot += 1
            slots.append(mine)
        loads.append((copies, slots))
    for copy in shared:
        copy.wait()
    stores = []
    for n, (_, parts) in enumerate(plan):
        copies, slots = loads[n]
        for copy in copies:
            copy.wait()
        for (col, _, out, row, out_col), mine in zip(parts, slots):
            total = lax.dot_general(
                grads[n], outs[:, col : col + WIDE], TN, preferred_element_type=jnp.float32
            )
            for k in mine:
                total = total + held[k].astype(jnp.float32)
            k = len(stores)
            sent[k] = total.astype(sent.dtype)
            copy = pltpu.make_async_copy(
                sent.at[k],
                results[out].at[row : row + BLK, out_col : out_col + WIDE],
                out_sems.at[k],
            )
            copy.start()
            stores.append(copy)
    for copy in stores:
        copy.wait()


def pieces(name, table, grads, outs, plan, arrived, out_shapes, after=()):
    tokens, cols = outs[0].shape
    parts = [part for _, each in plan for part in each]
    held = sum(len(part[1]) for part in parts)
    scratch = [
        pltpu.VMEM((2 * tokens, cols), jnp.bfloat16),
        pltpu.VMEM((len(plan), 2 * tokens, BLK), jnp.bfloat16),
    ]
    if held:
        scratch.append(pltpu.VMEM((held, BLK, WIDE), jnp.bfloat16))
    scratch += [
        pltpu.VMEM((len(parts), BLK, WIDE), jnp.bfloat16),
        pltpu.SemaphoreType.DMA((2 + 2 * len(plan) + held,)),
        pltpu.SemaphoreType.DMA((len(parts),)),
    ]
    operands = [*grads, *outs, *arrived, *after]
    return pl.pallas_call(
        lambda *refs: piece_kernel(plan, len(arrived), len(out_shapes), *refs),
        in_specs=[pl.BlockSpec(memory_space=pltpu.SMEM)]
        + [pl.BlockSpec(memory_space=pl.ANY)] * len(operands),
        out_specs=[pl.BlockSpec(memory_space=pl.ANY)] * len(out_shapes),
        out_shape=[jax.ShapeDtypeStruct(shape, jnp.bfloat16) for shape in out_shapes],
        scratch_shapes=scratch,
        compiler_params=params(),
        cost_estimate=cost(
            4 * tokens * BLK * WIDE * len(parts),
            2 * (2 * tokens * (cols + len(plan) * BLK) + (held + len(parts)) * BLK * WIDE),
        ),
        name=name,
    )(table, *operands)


def swap_halves(grad_rows, out_rows, core):
    grads = [grad_rows, swap_cores(other_half(grad_rows, core))]
    outs = [out_rows, swap_cores(out_rows)]
    return grads, outs


def first_stage(table, grads, outs, after):
    cols = outs[0].shape[1]
    plan = []
    for j in range(SIDE):
        row = j * BLK
        plan.append((SIDE * 2 + j, [(0, [], 0, row, 0), (WIDE, [], 1, row, 0)]))
        plan.append((SIDE * 1 + j, [(WIDE, [], 0, row, WIDE)]))
        plan.append((SIDE * 3 + j, [(0, [], 1, row, WIDE)]))
    plus, minus = pieces(
        "first_pieces", table, grads, outs, plan, [], [(SIDE * BLK, cols)] * 2, after
    )
    return hop(plus, 1), hop(minus, -1)


def second_stage(table, grads, outs, near, after):
    plan = []
    for j in range(SIDE):
        row = j * BLK
        plan.append((SIDE * 1 + j, [(0, [(0, j, 0)], 0, row, 0)]))
        plan.append((SIDE * 3 + j, [(WIDE, [(1, j, 0)], 1, row, 0)]))
    up, down = pieces(
        "second_pieces", table, grads, outs, plan, near, [(SIDE * BLK, WIDE)] * 2, after
    )
    return hop(up, 1), hop(down, -1)


def third_stage(table, grads, outs, near, far):
    plan = []
    for n in range(SIDE):
        at = (ORDER + n,)
        plan.append(
            (
                at,
                [
                    (0, [(2, at, 0), (1, at, WIDE)], n, 0, 0),
                    (WIDE, [(0, at, WIDE), (3, at, 0)], n, 0, WIDE),
                ],
            )
        )
    two, one, three, mine = pieces(
        "third_pieces", table, grads, outs, plan, [*near, *far], [(BLK, 2 * WIDE)] * SIDE
    )
    return mine, hop(two, 2, True), hop(one, 1, True), hop(three, -1, True)


def attend_kernel(
    low_ref, pos_ref, q_ref, g_ref, o_ref, key_ref, val_ref,
    kv4, kv3, kv2, kv1,
    packed_ref, own_ref, back4, back3, back2, back1,
    bias, held, keys, keys_t, vals, dkey, dval,
):
    step = pl.program_id(0)
    scale = 1.0 / math.sqrt(HEAD)
    tiles = RUN // TILE

    @pl.when(step == 0)
    def _():
        for t in range(tiles):
            row = lax.broadcasted_iota(jnp.int32, (SEEN, TILE), 0)
            col = lax.broadcasted_iota(jnp.int32, (SEEN, TILE), 1)
            low = low_ref[:, t * TILE : (t + 1) * TILE] - t * TILE
            one = jnp.where((row >= low) & (row <= col + BACK * RUN), 0.0, NEG)
            for h in range(STACK):
                bias[t, :, h * TILE : (h + 1) * TILE] = one
        for n, ref in enumerate((kv4, kv3, kv2, kv1)):
            keys[n * RUN : (n + 1) * RUN, :] = ref[:, :HEAD]
            vals[n * RUN : (n + 1) * RUN, :] = ref[:, HEAD:]
        keys[BACK * RUN :, :] = key_ref[...]
        vals[BACK * RUN :, :] = val_ref[...]
        keys_t[...] = keys[...].T
        dkey[...] = jnp.zeros_like(dkey)
        dval[...] = jnp.zeros_like(dval)

    def begin(t):
        rows = slice(t * TILE, (t + 1) * TILE)

        def stack(ref):
            return jnp.concatenate(
                [ref[rows, h * HEAD : (h + 1) * HEAD] for h in range(STACK)], axis=0
            )

        q, g = stack(q_ref), stack(g_ref)
        prod = g.astype(jnp.float32) * stack(o_ref).astype(jnp.float32)
        row_dot = jnp.sum(prod.T, axis=0, keepdims=True)
        top = jnp.full((1, STACK * TILE), 2 * NEG, jnp.float32)
        for at in range(0, SEEN, CHUNK):
            seen = slice(t * TILE + at, t * TILE + at + CHUNK)
            scores = lax.dot_general(keys[seen, :], q, NT, preferred_element_type=jnp.float32)
            scores = scores * (scale * math.log2(math.e)) + bias[t, at : at + CHUNK, :]
            held[t, at : at + CHUNK, :] = scores
            top = jnp.maximum(top, jnp.max(scores, axis=0, keepdims=True))
        return q, g, row_dot, top

    def exponents(t, top):
        total = jnp.zeros_like(top)
        for at in range(0, SEEN, CHUNK):
            probs = jnp.exp2(held[t, at : at + CHUNK, :] - top)
            held[t, at : at + CHUNK, :] = probs
            total = total + jnp.sum(probs, axis=0, keepdims=True)
        return 1.0 / total

    def finish(t, q, g, row_dot, inverse):
        dq_t = jnp.zeros((HEAD, STACK * TILE), jnp.float32)
        for at in range(0, SEEN, CHUNK):
            seen = slice(t * TILE + at, t * TILE + at + CHUNK)
            probs = held[t, at : at + CHUNK, :] * inverse
            dval[seen, :] += jnp.dot(
                probs.astype(jnp.bfloat16), g, preferred_element_type=jnp.float32
            )
            prob_grad = lax.dot_general(vals[seen, :], g, NT, preferred_element_type=jnp.float32)
            score_grad = (probs * (prob_grad - row_dot)).astype(jnp.bfloat16)
            dkey[seen, :] += jnp.dot(score_grad, q, preferred_element_type=jnp.float32)
            dq_t += jnp.dot(keys_t[:, seen], score_grad, preferred_element_type=jnp.float32)
        return (dq_t * scale).T.astype(jnp.bfloat16)

    grads = []
    unit = begin(0)
    for t in range(tiles):
        q, g, row_dot, top = unit
        inverse = exponents(t, top)
        if t + 1 < tiles:
            unit = begin(t + 1)
        grads.append(finish(t, q, g, row_dot, inverse))
    slots = lax.broadcasted_iota(jnp.int32, (packed_ref.shape[0], RUN), 0)
    select = (slots == pos_ref[...]).astype(jnp.bfloat16)
    dq = jnp.concatenate(
        [
            jnp.concatenate([part[h * TILE : (h + 1) * TILE, :] for part in grads], axis=0)
            for h in range(STACK)
        ],
        axis=1,
    )
    packed_ref[...] = jnp.dot(select, dq, preferred_element_type=jnp.float32).astype(jnp.bfloat16)

    @pl.when(step == pl.num_programs(0) - 1)
    def _():
        for n, ref in enumerate((back4, back3, back2, back1)):
            rows = slice(n * RUN, (n + 1) * RUN)
            ref[:, :HEAD] = (dkey[rows, :] * scale).astype(jnp.bfloat16)
            ref[:, HEAD:] = dval[rows, :].astype(jnp.bfloat16)
        own_ref[:, :HEAD] = dkey[BACK * RUN :, :] * scale
        own_ref[:, HEAD:] = dval[BACK * RUN :, :]


def attend(low, pos, query, grad, out, key, value, earlier, slots):
    heads = query.shape[1] // HEAD
    window = (BACK + 1) * RUN
    whole = lambda shape: pl.BlockSpec(shape, lambda h: (0, 0))
    by_heads = lambda rows: pl.BlockSpec((rows, STACK * HEAD), lambda h: (0, h))
    pair = (RUN, 2 * HEAD)
    return pl.pallas_call(
        attend_kernel,
        grid=(heads // STACK,),
        in_specs=[whole((1, RUN))] * 2
        + [by_heads(RUN)] * 3
        + [whole((RUN, HEAD))] * 2
        + [whole(pair)] * BACK,
        out_specs=[by_heads(slots), whole(pair)] + [whole(pair)] * BACK,
        out_shape=[
            jax.ShapeDtypeStruct((slots, query.shape[1]), jnp.bfloat16),
            jax.ShapeDtypeStruct(pair, jnp.float32),
        ]
        + [jax.ShapeDtypeStruct(pair, jnp.bfloat16)] * BACK,
        scratch_shapes=[
            pltpu.VMEM((RUN // TILE, SEEN, STACK * TILE), jnp.float32),
            pltpu.VMEM((RUN // TILE, SEEN, STACK * TILE), jnp.float32),
            pltpu.VMEM((window, HEAD), jnp.bfloat16),
            pltpu.VMEM((HEAD, window), jnp.bfloat16),
            pltpu.VMEM((window, HEAD), jnp.bfloat16),
            pltpu.VMEM((window, HEAD), jnp.float32),
            pltpu.VMEM((window, HEAD), jnp.float32),
        ],
        compiler_params=params(),
        cost_estimate=cost(10 * heads * RUN * window * HEAD, 8 * MIB, heads * RUN * window),
        name="attend",
    )(low, pos, query, grad, out, key, value, *earlier)


def route_rows(slot_blocks, own_index, parties, block_rows):
    total = slot_blocks.shape[0]
    ids = jnp.arange(total, dtype=jnp.int32)
    slot_of_block = jnp.sum(
        jnp.where(slot_blocks[None, :] == ids[:, None], ids[None, :], 0), axis=1
    )
    local = jnp.arange(parties, dtype=jnp.int32)

    def place(peer, order):
        earlier = (peer[:, None] == peer[None, :]) & (order[None, :] < order[:, None])
        return peer * CAP + jnp.sum(earlier, axis=1).astype(jnp.int32)

    dest_slot = lax.dynamic_slice_in_dim(slot_of_block, own_index * parties, parties, 0)
    held = lax.dynamic_slice_in_dim(slot_blocks, own_index * parties, parties, 0)
    rows = jnp.arange(block_rows, dtype=jnp.int32)

    def spread(at):
        return (at[:, None] * block_rows + rows[None, :]).reshape(-1)

    return spread(place(dest_slot // parties, dest_slot)), spread(place(held // parties, local))


def on_device(
    grad_out, out_weight, query_states, key_states, value_tensor, attn_out, doc_ids, block_order
):
    parties = lax.axis_size("ctx")
    own_index = lax.axis_index("ctx")
    core = lax.axis_index("dp")
    x, y = own_index // SIDE, own_index % SIDE
    grad_rows, out_rows = grad_out[0], attn_out[0]
    doc_row = doc_ids[0]
    key, value = key_states[0], value_tensor[0]

    both = jnp.concatenate([key, value], axis=1)
    earlier = [lax.ppermute(both, "ctx", run_shift(k, parties)) for k in range(BACK, 0, -1)]

    table = block_table(x, y, core)
    grads, outs = swap_halves(grad_rows, out_rows, core)
    near = first_stage(table, grads, outs, earlier)

    attn_grad = project(grad_rows, out_weight)
    own_docs = lax.dynamic_slice_in_dim(doc_row, own_index * RUN, RUN, 0)
    start = jnp.maximum(own_index - BACK, 0) * RUN
    seen_docs = lax.dynamic_slice_in_dim(doc_row, start, (BACK + 1) * RUN, 0)
    first = start + jnp.sum((seen_docs[:, None] < own_docs[None, :]).astype(jnp.int32), axis=0)
    low = (first - (own_index - BACK) * RUN).reshape(1, RUN)
    send_rows, held_rows = route_rows(block_order[0], own_index, parties, RUN // parties)
    slots = CAP * RUN
    packed, own_kv, *back = attend(
        low,
        send_rows.reshape(1, RUN),
        query_states[0],
        attn_grad,
        out_rows,
        key,
        value,
        earlier,
        slots,
    )
    far = second_stage(table, grads, outs, near, [own_kv])
    got = lax.all_to_all(
        packed.reshape(parties, slots // parties, -1), "ctx", 0, 0, tiled=True
    ).reshape(slots, -1)
    held_select = (
        held_rows[:, None] == jnp.arange(slots, dtype=jnp.int32)[None, :]
    ).astype(jnp.bfloat16)
    query_grad = jnp.dot(held_select, got, preferred_element_type=jnp.float32).astype(jnp.bfloat16)
    returned = [
        lax.ppermute(v, "ctx", run_shift(-k, parties)) for v, k in zip(back, range(BACK, 0, -1))
    ]
    kv_sum = own_kv
    for v in returned:
        kv_sum = kv_sum + v.astype(jnp.float32)
    kv_sum = kv_sum.astype(jnp.bfloat16)
    mine, *others = third_stage(table, grads, outs, near, far)
    weight_grad = mine.astype(jnp.float32)
    for v in others:
        weight_grad = weight_grad + v.astype(jnp.float32)
    return (
        query_grad[None],
        kv_sum[None, :, :HEAD],
        kv_sum[None, :, HEAD:],
        weight_grad,
    )


def solution(mesh):
    heads = P("dp", "ctx", "tp")
    in_specs = (
        P("dp", "ctx", None),
        P(None, "tp"),
        heads,
        heads,
        heads,
        heads,
        P("dp", None),
        P("dp", None),
    )
    out_specs = (heads, heads, heads, P(("ctx", "dp"), "tp"))
    return jax.shard_map(
        on_device, mesh=mesh, in_specs=in_specs, out_specs=out_specs, check_vma=False
    )
```

```python
import math

import jax
import jax.numpy as jnp
from jax import lax
from jax.experimental import pallas as pl
from jax.experimental.pallas import tpu as pltpu
from jax.sharding import PartitionSpec as P

HEAD = 128
CAP = 2
SIDE = 4
BACK = 4
RUN = 256
BLK = 256
TILE = 128
SEEN = BACK * RUN + TILE
CHUNK = 384
PIECES_MIB = 24
WIDE = 512
NEG = -1e30
MIB = 1024 * 1024
NT = (((1,), (1,)), ((), ()))
TN = (((0,), (0,)), ((), ()))


def run_shift(k, parties):
    return [(i, (i + k) % parties) for i in range(parties)]


def axis_shift(k, second):
    pairs = []
    for x in range(SIDE):
        for y in range(SIDE):
            for core in range(2):
                along_x = (core == 0) != second
                to_x, to_y = ((x + k) % SIDE, y) if along_x else (x, (y + k) % SIDE)
                pairs.append(((x * SIDE + y) * 2 + core, (to_x * SIDE + to_y) * 2 + core))
    return pairs


def hop(value, k, second=False):
    return lax.ppermute(value, ("ctx", "dp"), axis_shift(k, second))


def swap_cores(value):
    return lax.ppermute(value, "dp", [(0, 1), (1, 0)])


def params(mib):
    return pltpu.CompilerParams(vmem_limit_bytes=mib * MIB)


def hbm(values):
    return [pltpu.with_memory_space_constraint(v, pltpu.HBM) for v in values]


def cost(flops, moved, exps=0):
    return pl.CostEstimate(flops=flops, bytes_accessed=moved, transcendentals=exps)


def project_kernel(grad_ref, weight_ref, after_ref, out_ref, grads, weights, grad_sems, weight_sems):
    slabs = grad_sems.shape[0]
    depth = weight_ref.shape[0] // slabs
    copies = []
    for i in range(slabs):
        part = slice(i * depth, (i + 1) * depth)
        copies.append(
            (
                pltpu.make_async_copy(grad_ref.at[:, part], grads.at[:, part], grad_sems.at[i]),
                pltpu.make_async_copy(weight_ref.at[part], weights.at[part], weight_sems.at[i]),
            )
        )
    for pair in copies:
        for copy in pair:
            copy.start()
    total = None
    for i, pair in enumerate(copies):
        for copy in pair:
            copy.wait()
        part = slice(i * depth, (i + 1) * depth)
        addend = jnp.dot(grads[:, part], weights[part, :], preferred_element_type=jnp.float32)
        total = addend if total is None else total + addend
    out_ref[...] = total.astype(out_ref.dtype)


def project(grad_rows, weight, after):
    rows, depth = grad_rows.shape
    cols = weight.shape[1]
    slabs = 8
    return pl.pallas_call(
        project_kernel,
        in_specs=[pl.BlockSpec(memory_space=pl.ANY)] * 3,
        out_specs=pl.BlockSpec(memory_space=pltpu.VMEM),
        out_shape=jax.ShapeDtypeStruct((rows, cols), jnp.bfloat16),
        scratch_shapes=[
            pltpu.VMEM(grad_rows.shape, grad_rows.dtype),
            pltpu.VMEM(weight.shape, weight.dtype),
            pltpu.SemaphoreType.DMA((slabs,)),
            pltpu.SemaphoreType.DMA((slabs,)),
        ],
        compiler_params=params(32),
        cost_estimate=cost(2 * rows * depth * cols, 2 * depth * (rows + cols)),
        name="project",
    )(*hbm([grad_rows, weight]), after)


def block_table(x, y, core):
    first, second = jnp.where(core == 0, x, y), jnp.where(core == 0, y, x)
    step_first, step_second = jnp.where(core == 0, SIDE, 1), jnp.where(core == 0, 1, SIDE)
    offsets = jnp.arange(SIDE, dtype=jnp.int32)
    blocks = ((first + offsets[:, None]) % SIDE) * step_first + offsets[None, :] * step_second
    order = (second + jnp.stack([jnp.int32(v) for v in (2, 1, 3, 0)])) % SIDE
    table = jnp.concatenate([blocks.reshape(-1), order, core.reshape(1)])
    return table.astype(jnp.int32)


ORDER, CORE = SIDE * SIDE, SIDE * SIDE + SIDE


def turn_kernel(*refs):
    refs[-1][...] = refs[0][...].T


def turn(value, after):
    rows, cols = value.shape
    return pl.pallas_call(
        turn_kernel,
        in_specs=[pl.BlockSpec(memory_space=pltpu.VMEM), pl.BlockSpec(memory_space=pl.ANY)],
        out_specs=pl.BlockSpec(memory_space=pltpu.VMEM),
        out_shape=jax.ShapeDtypeStruct((cols, rows), value.dtype),
        compiler_params=params(8),
        cost_estimate=cost(0, 4 * rows * cols),
        name="turn",
    )(value, after)


def piece_kernel(plan, arrived_count, out_count, extra, blocks, *refs):
    grad_refs, out_refs = refs[:2], refs[2:4]
    arrived_refs = refs[4 : 4 + arrived_count]
    refs = refs[4 + arrived_count + extra :]
    results, refs = refs[:out_count], refs[out_count:]
    if arrived_count:
        outs, grads, held, sent, in_sems, out_sems = refs
    else:
        outs, grads, sent, in_sems, out_sems = refs
    tokens = out_refs[0].shape[1]
    core = blocks[CORE]
    taken = 0

    def load(source, target):
        nonlocal taken
        copy = pltpu.make_async_copy(source, target, in_sems.at[taken])
        taken += 1
        copy.start()
        return copy

    def number(at):
        return blocks[at] if isinstance(at, int) else blocks[blocks[at[0]]]

    shared = [
        load(ref, outs.at[:, n * tokens : (n + 1) * tokens]) for n, ref in enumerate(out_refs)
    ]

    def fetch(n, slot):
        at, parts = plan[n]
        copies = []
        for j, place in enumerate(at):
            first = pl.multiple_of((2 * number(place) + core) * BLK, BLK)
            for k, ref in enumerate(grad_refs):
                copies.append(
                    load(
                        ref.at[:, pl.ds(first, BLK)],
                        grads.at[n, k * tokens : (k + 1) * tokens, j * BLK : (j + 1) * BLK],
                    )
                )
        slots = []
        for _, arrived, _ in parts:
            mine = []
            for which, row, places in arrived:
                rows = arrived_refs[which].at[row : row + WIDE]
                if places is None:
                    copies.append(load(rows, held.at[slot]))
                else:
                    for j, place in enumerate(places):
                        first = pl.multiple_of(blocks[place] * BLK, BLK)
                        copies.append(
                            load(
                                rows.at[:, pl.ds(first, BLK)],
                                held.at[slot, :, j * BLK : (j + 1) * BLK],
                            )
                        )
                mine.append(slot)
                slot += 1
            slots.append(mine)
        return copies, slots, slot

    ahead = fetch(0, 0)
    for copy in shared:
        copy.wait()
    stores, done = [], 0
    for n, (_, parts) in enumerate(plan):
        copies, slots, slot = ahead
        if n + 1 < len(plan):
            ahead = fetch(n + 1, slot)
        for copy in copies:
            copy.wait()
        for (col, _, targets), mine in zip(parts, slots):
            total = jnp.dot(
                outs[col : col + WIDE, :], grads[n], preferred_element_type=jnp.float32
            )
            for k in mine:
                total = total + held[k].astype(jnp.float32)
            sent[done] = total.astype(sent.dtype)
            for out, row, first, count in targets:
                copy = pltpu.make_async_copy(
                    sent.at[done, :, first : first + count],
                    results[out].at[row : row + WIDE],
                    out_sems.at[len(stores)],
                )
                copy.start()
                stores.append(copy)
            done += 1
    for copy in stores:
        copy.wait()


def pieces(name, table, grads, outs, plan, arrived, out_shapes, after=()):
    cols, tokens = outs[0].shape
    parts = [part for _, each in plan for part in each]
    terms = [term for part in parts for term in part[1]]
    loads = 2 + 2 * sum(len(at) for at, _ in plan)
    loads += sum(1 if term[2] is None else len(term[2]) for term in terms)
    rows = SIDE * BLK
    scratch = [
        pltpu.VMEM((cols, 2 * tokens), jnp.bfloat16),
        pltpu.VMEM((len(plan), 2 * tokens, rows), jnp.bfloat16),
    ]
    if terms:
        scratch.append(pltpu.VMEM((len(terms), WIDE, rows), jnp.bfloat16))
    scratch += [
        pltpu.VMEM((len(parts), WIDE, rows), jnp.bfloat16),
        pltpu.SemaphoreType.DMA((loads,)),
        pltpu.SemaphoreType.DMA((sum(len(part[2]) for part in parts),)),
    ]
    operands = [*grads, *outs, *arrived, *after]
    return pl.pallas_call(
        lambda *refs: piece_kernel(plan, len(arrived), len(out_shapes), len(after), *refs),
        in_specs=[pl.BlockSpec(memory_space=pltpu.SMEM)]
        + [pl.BlockSpec(memory_space=pl.ANY)] * len(operands),
        out_specs=[pl.BlockSpec(memory_space=pl.ANY)] * len(out_shapes),
        out_shape=[pltpu.HBM(shape, jnp.bfloat16) for shape in out_shapes],
        scratch_shapes=scratch,
        compiler_params=params(PIECES_MIB),
        cost_estimate=cost(
            4 * tokens * rows * WIDE * len(parts),
            2 * (2 * tokens * (cols + len(plan) * rows) + (len(terms) + len(parts)) * rows * WIDE),
        ),
        name=name,
    )(table, *hbm(operands[:1]), *operands[1:])


def chunk(k):
    return [SIDE * k + j for j in range(SIDE)]


def far_stage(table, grads, outs, after):
    rows = SIDE * BLK
    plan = [(chunk(2), [(0, [], [(0, 0, 0, rows)]), (WIDE, [], [(1, 0, 0, rows)])])]
    plus, minus = pieces("far_pieces", table, grads, outs, plan, [], [(WIDE, rows)] * 2, after)
    return hop(plus, 1), hop(minus, -1)


def near_stage(table, grads, outs, after):
    rows = SIDE * BLK
    plan = [
        (chunk(1), [(WIDE, [], [(0, 0, 0, rows)])]),
        (chunk(3), [(0, [], [(1, 0, 0, rows)])]),
    ]
    plus, minus = pieces("near_pieces", table, grads, outs, plan, [], [(WIDE, rows)] * 2, after)
    return [hop(plus, 1), hop(minus, -1)], [plus, minus]


def join_stage(table, grads, outs, far, after):
    rows = SIDE * BLK
    plan = [
        (chunk(1), [(0, [(0, 0, None)], [(0, 0, 0, rows)])]),
        (chunk(3), [(WIDE, [(1, 0, None)], [(1, 0, 0, rows)])]),
    ]
    up, down = pieces("join_pieces", table, grads, outs, plan, far, [(WIDE, rows)] * 2, after)
    return [hop(up, 1), hop(down, -1)], [up, down]


def block_stage(table, grads, outs, near, joined):
    places = [ORDER + n for n in range(SIDE)]
    left = [(n, 0, n * BLK, BLK) for n in range(SIDE)]
    right = [(n, WIDE, n * BLK, BLK) for n in range(SIDE)]
    plan = [
        (
            [(place,) for place in places],
            [
                (0, [(2, 0, places), (1, 0, places)], left),
                (WIDE, [(0, 0, places), (3, 0, places)], right),
            ],
        )
    ]
    two, one, three, mine = pieces(
        "block_pieces", table, grads, outs, plan, [*near, *joined], [(2 * WIDE, BLK)] * SIDE
    )
    return mine, hop(two, 2, True), hop(one, 1, True), hop(three, -1, True)


def total_kernel(*refs):
    total = refs[0][...].astype(jnp.float32)
    for ref in refs[1:-1]:
        total = total + ref[...].astype(jnp.float32)
    refs[-1][...] = total.T


def total_gradient(terms):
    cols, rows = terms[0].shape
    return pl.pallas_call(
        total_kernel,
        in_specs=[pl.BlockSpec(memory_space=pltpu.VMEM)] * len(terms),
        out_specs=pl.BlockSpec(memory_space=pltpu.VMEM),
        out_shape=jax.ShapeDtypeStruct((rows, cols), jnp.float32),
        compiler_params=params(16),
        cost_estimate=cost(4 * rows * cols, 12 * rows * cols),
        name="total_gradient",
    )(*hbm(terms[:1]), *terms[1:])


def attend_kernel(
    low_ref, pos_ref, q_ref, g_ref, o_ref, key_ref, val_ref,
    kv4, kv3, kv2, kv1, after_plus, after_minus,
    packed_ref, own_ref, back4, back3, back2, back1,
    bias, held, keys, keys_t, vals, dkey, dval,
):
    tile = pl.program_id(0)
    scale = 1.0 / math.sqrt(HEAD)
    heads = q_ref.shape[1] // HEAD
    width = heads * TILE
    first = pl.multiple_of(tile * TILE, TILE)

    @pl.when(tile == 0)
    def _():
        for n, ref in enumerate((kv4, kv3, kv2, kv1)):
            keys[n * RUN : (n + 1) * RUN, :] = ref[:, :HEAD]
            vals[n * RUN : (n + 1) * RUN, :] = ref[:, HEAD:]
        keys[BACK * RUN :, :] = key_ref[...]
        vals[BACK * RUN :, :] = val_ref[...]
        keys_t[...] = keys[...].T
        dkey[...] = jnp.zeros_like(dkey)
        dval[...] = jnp.zeros_like(dval)

    row = lax.broadcasted_iota(jnp.int32, (SEEN, TILE), 0)
    col = lax.broadcasted_iota(jnp.int32, (SEEN, TILE), 1)
    low = low_ref[...] - first
    bias[...] = jnp.where((row >= low) & (row <= col + BACK * RUN), 0.0, NEG)

    def stack(ref):
        return jnp.concatenate([ref[:, h * HEAD : (h + 1) * HEAD] for h in range(heads)], axis=0)

    q, g = stack(q_ref), stack(g_ref)
    dots = []
    for h in range(heads):
        part = slice(h * HEAD, (h + 1) * HEAD)
        prod = g_ref[:, part].astype(jnp.float32) * o_ref[:, part].astype(jnp.float32)
        dots.append(jnp.sum(prod.T, axis=0, keepdims=True))
    row_dot = jnp.concatenate(dots, axis=1)
    top = jnp.full((1, width), 2 * NEG, jnp.float32)
    for at in range(0, SEEN, CHUNK):
        rows = pl.ds(pl.multiple_of(first + at, TILE), CHUNK)
        scores = lax.dot_general(keys[rows, :], q, NT, preferred_element_type=jnp.float32)
        mask = jnp.concatenate([bias[at : at + CHUNK, :]] * heads, axis=1)
        scores = scores * (scale * math.log2(math.e)) + mask
        held[at : at + CHUNK, :] = scores
        top = jnp.maximum(top, jnp.max(scores, axis=0, keepdims=True))
    total = jnp.zeros((1, width), jnp.float32)
    for at in range(0, SEEN, CHUNK):
        probs = jnp.exp2(held[at : at + CHUNK, :] - top)
        held[at : at + CHUNK, :] = probs
        total = total + jnp.sum(probs, axis=0, keepdims=True)
    inverse = 1.0 / total
    dq_t = jnp.zeros((HEAD, width), jnp.float32)
    for at in range(0, SEEN, CHUNK):
        rows = pl.ds(pl.multiple_of(first + at, TILE), CHUNK)
        probs = held[at : at + CHUNK, :] * inverse
        dval[rows, :] += jnp.dot(probs.astype(jnp.bfloat16), g, preferred_element_type=jnp.float32)
        prob_grad = lax.dot_general(vals[rows, :], g, NT, preferred_element_type=jnp.float32)
        score_grad = (probs * (prob_grad - row_dot)).astype(jnp.bfloat16)
        dkey[rows, :] += jnp.dot(score_grad, q, preferred_element_type=jnp.float32)
        dq_t += jnp.dot(keys_t[:, rows], score_grad, preferred_element_type=jnp.float32)
    dq_t = dq_t * scale
    dq = jnp.concatenate(
        [dq_t[:, h * TILE : (h + 1) * TILE].T for h in range(heads)], axis=1
    ).astype(jnp.bfloat16)
    slots = lax.broadcasted_iota(jnp.int32, (packed_ref.shape[0], TILE), 0)
    select = (slots == pos_ref[...]).astype(jnp.bfloat16)
    placed = jnp.dot(select, dq, preferred_element_type=jnp.float32).astype(jnp.bfloat16)

    @pl.when(tile == 0)
    def _():
        packed_ref[...] = placed

    @pl.when(tile > 0)
    def _():
        packed_ref[...] += placed

    @pl.when(tile == pl.num_programs(0) - 1)
    def _():
        for n, ref in enumerate((back4, back3, back2, back1)):
            rows = slice(n * RUN, (n + 1) * RUN)
            ref[:, :HEAD] = (dkey[rows, :] * scale).astype(jnp.bfloat16)
            ref[:, HEAD:] = dval[rows, :].astype(jnp.bfloat16)
        own_ref[:, :HEAD] = dkey[BACK * RUN :, :] * scale
        own_ref[:, HEAD:] = dval[BACK * RUN :, :]


def attend(low, pos, query, grad, out, key, value, earlier, slots, after):
    cols = query.shape[1]
    heads = cols // HEAD
    window = (BACK + 1) * RUN
    whole = lambda shape: pl.BlockSpec(shape, lambda t: (0, 0))
    by_tile = pl.BlockSpec((TILE, cols), lambda t: (t, 0))
    pair = (RUN, 2 * HEAD)
    return pl.pallas_call(
        attend_kernel,
        grid=(RUN // TILE,),
        in_specs=[pl.BlockSpec((1, TILE), lambda t: (0, t))] * 2
        + [by_tile] * 3
        + [whole((RUN, HEAD))] * 2
        + [whole(pair)] * BACK
        + [pl.BlockSpec(memory_space=pl.ANY)] * len(after),
        out_specs=[whole((slots, cols)), whole(pair)] + [whole(pair)] * BACK,
        out_shape=[
            pltpu.HBM((slots, cols), jnp.bfloat16),
            pltpu.HBM(pair, jnp.float32),
        ]
        + [pltpu.HBM(pair, jnp.bfloat16)] * BACK,
        scratch_shapes=[
            pltpu.VMEM((SEEN, TILE), jnp.float32),
            pltpu.VMEM((SEEN, heads * TILE), jnp.float32),
            pltpu.VMEM((window, HEAD), jnp.bfloat16),
            pltpu.VMEM((HEAD, window), jnp.bfloat16),
            pltpu.VMEM((window, HEAD), jnp.bfloat16),
            pltpu.VMEM((window, HEAD), jnp.float32),
            pltpu.VMEM((window, HEAD), jnp.float32),
        ],
        compiler_params=params(32),
        cost_estimate=cost(10 * heads * RUN * window * HEAD, 8 * MIB, heads * RUN * window),
        name="attend",
    )(*hbm([low, pos, query]), grad, *hbm([out, key, value]), *earlier, *after)


def route_rows(slot_blocks, own_index, parties, block_rows):
    total = slot_blocks.shape[0]
    ids = jnp.arange(total, dtype=jnp.int32)
    slot_of_block = jnp.sum(
        jnp.where(slot_blocks[None, :] == ids[:, None], ids[None, :], 0), axis=1
    )
    local = jnp.arange(parties, dtype=jnp.int32)

    def place(peer, order):
        earlier = (peer[:, None] == peer[None, :]) & (order[None, :] < order[:, None])
        return peer * CAP + jnp.sum(earlier, axis=1).astype(jnp.int32)

    dest_slot = lax.dynamic_slice_in_dim(slot_of_block, own_index * parties, parties, 0)
    held = lax.dynamic_slice_in_dim(slot_blocks, own_index * parties, parties, 0)
    rows = jnp.arange(block_rows, dtype=jnp.int32)

    def spread(at):
        return (at[:, None] * block_rows + rows[None, :]).reshape(-1)

    return spread(place(dest_slot // parties, dest_slot)), spread(place(held // parties, local))


def on_device(
    grad_out, out_weight, query_states, key_states, value_tensor, attn_out, doc_ids, block_order
):
    parties = lax.axis_size("ctx")
    own_index = lax.axis_index("ctx")
    core = lax.axis_index("dp")
    x, y = own_index // SIDE, own_index % SIDE
    grad_rows, out_rows = grad_out[0], attn_out[0]
    doc_row = doc_ids[0]
    key, value = key_states[0], value_tensor[0]

    both = jnp.concatenate([key, value], axis=1)
    earlier = [lax.ppermute(both, "ctx", run_shift(k, parties)) for k in range(BACK, 0, -1)]

    table = block_table(x, y, core)
    grads = [grad_rows, swap_cores(grad_rows)]
    turned = turn(out_rows, grads[1])
    outs = [turned, swap_cores(turned)]
    attn_grad = project(grad_rows, out_weight, turned)
    far = far_stage(table, grads, outs, [*earlier, attn_grad])
    near, near_sent = near_stage(table, grads, outs, [attn_grad])
    joined, joined_sent = join_stage(table, grads, outs, far, hbm(near_sent))
    own_docs = lax.dynamic_slice_in_dim(doc_row, own_index * RUN, RUN, 0)
    start = jnp.maximum(own_index - BACK, 0) * RUN
    seen_docs = lax.dynamic_slice_in_dim(doc_row, start, (BACK + 1) * RUN, 0)
    first = start + jnp.sum((seen_docs[:, None] < own_docs[None, :]).astype(jnp.int32), axis=0)
    low = (first - (own_index - BACK) * RUN).reshape(1, RUN)
    send_rows, held_rows = route_rows(block_order[0], own_index, parties, RUN // parties)
    slots = CAP * RUN
    packed, own_kv, *back = attend(
        low,
        send_rows.reshape(1, RUN),
        query_states[0],
        attn_grad,
        out_rows,
        key,
        value,
        earlier,
        slots,
        hbm(joined_sent),
    )
    got = lax.all_to_all(
        packed.reshape(parties, slots // parties, -1), "ctx", 0, 0, tiled=True
    ).reshape(slots, -1)
    held_select = (
        held_rows[:, None] == jnp.arange(slots, dtype=jnp.int32)[None, :]
    ).astype(jnp.bfloat16)
    query_grad = jnp.dot(held_select, got, preferred_element_type=jnp.float32).astype(jnp.bfloat16)
    returned = [
        lax.ppermute(v, "ctx", run_shift(-k, parties)) for v, k in zip(back, range(BACK, 0, -1))
    ]
    kv_sum = own_kv
    for v in returned:
        kv_sum = kv_sum + v.astype(jnp.float32)
    kv_sum = kv_sum.astype(jnp.bfloat16)
    weight_grad = total_gradient(block_stage(table, grads, outs, near, joined))
    return (
        query_grad[None],
        kv_sum[None, :, :HEAD],
        kv_sum[None, :, HEAD:],
        weight_grad,
    )


def solution(mesh):
    heads = P("dp", "ctx", "tp")
    in_specs = (
        P("dp", "ctx", None),
        P(None, "tp"),
        heads,
        heads,
        heads,
        heads,
        P("dp", None),
        P("dp", None),
    )
    out_specs = (heads, heads, heads, P(("ctx", "dp"), "tp"))
    return jax.shard_map(
        on_device, mesh=mesh, in_specs=in_specs, out_specs=out_specs, check_vma=False
    )
```

```python
import math

import jax
import jax.numpy as jnp
from jax import lax
from jax.experimental import pallas as pl
from jax.experimental.pallas import tpu as pltpu
from jax.sharding import PartitionSpec as P

HEAD = 128
CAP = 2
SIDE = 4
BACK = 4
RUN = 256
BLK = 256
TILE = 128
SEEN = BACK * RUN + TILE
CHUNK = 1152
PIECES_MIB = 24
WIDE = 512
PAIR = 2 * HEAD
NEG = -1e30
MIB = 1024 * 1024
NT = (((1,), (1,)), ((), ()))
TN = (((0,), (0,)), ((), ()))


def run_shift(k, parties):
    return [(i, (i + k) % parties) for i in range(parties)]


def axis_shift(k, second):
    pairs = []
    for x in range(SIDE):
        for y in range(SIDE):
            for core in range(2):
                along_x = (core == 0) != second
                to_x, to_y = ((x + k) % SIDE, y) if along_x else (x, (y + k) % SIDE)
                pairs.append(((x * SIDE + y) * 2 + core, (to_x * SIDE + to_y) * 2 + core))
    return pairs


def hop(value, k, second=False):
    return lax.ppermute(value, ("ctx", "dp"), axis_shift(k, second))


def swap_cores(value):
    return lax.ppermute(value, "dp", [(0, 1), (1, 0)])


def params(mib):
    return pltpu.CompilerParams(vmem_limit_bytes=mib * MIB)


def hbm(values):
    return [pltpu.with_memory_space_constraint(v, pltpu.HBM) for v in values]


def cost(flops, moved, exps=0):
    return pl.CostEstimate(flops=flops, bytes_accessed=moved, transcendentals=exps)


def project_kernel(grad_ref, weight_ref, after_ref, out_ref, grads, weights, grad_sems, weight_sems):
    slabs = grad_sems.shape[0]
    depth = weight_ref.shape[0] // slabs
    copies = []
    for i in range(slabs):
        part = slice(i * depth, (i + 1) * depth)
        copies.append(
            (
                pltpu.make_async_copy(grad_ref.at[:, part], grads.at[:, part], grad_sems.at[i]),
                pltpu.make_async_copy(weight_ref.at[part], weights.at[part], weight_sems.at[i]),
            )
        )
    for pair in copies:
        for copy in pair:
            copy.start()
    total = None
    for i, pair in enumerate(copies):
        for copy in pair:
            copy.wait()
        part = slice(i * depth, (i + 1) * depth)
        addend = jnp.dot(grads[:, part], weights[part, :], preferred_element_type=jnp.float32)
        total = addend if total is None else total + addend
    out_ref[...] = total.astype(out_ref.dtype)


def project(grad_rows, weight, after):
    rows, depth = grad_rows.shape
    cols = weight.shape[1]
    slabs = 8
    return pl.pallas_call(
        project_kernel,
        in_specs=[pl.BlockSpec(memory_space=pl.ANY)] * 3,
        out_specs=pl.BlockSpec(memory_space=pltpu.VMEM),
        out_shape=jax.ShapeDtypeStruct((rows, cols), jnp.bfloat16),
        scratch_shapes=[
            pltpu.VMEM(grad_rows.shape, grad_rows.dtype),
            pltpu.VMEM(weight.shape, weight.dtype),
            pltpu.SemaphoreType.DMA((slabs,)),
            pltpu.SemaphoreType.DMA((slabs,)),
        ],
        compiler_params=params(32),
        cost_estimate=cost(2 * rows * depth * cols, 2 * depth * (rows + cols)),
        name="project",
    )(*hbm([grad_rows, weight]), after)


def block_table(x, y, core):
    first, second = jnp.where(core == 0, x, y), jnp.where(core == 0, y, x)
    step_first, step_second = jnp.where(core == 0, SIDE, 1), jnp.where(core == 0, 1, SIDE)
    offsets = jnp.arange(SIDE, dtype=jnp.int32)
    blocks = ((first + offsets[:, None]) % SIDE) * step_first + offsets[None, :] * step_second
    order = (second + jnp.stack([jnp.int32(v) for v in (2, 1, 3, 0)])) % SIDE
    table = jnp.concatenate([blocks.reshape(-1), order, core.reshape(1)])
    return table.astype(jnp.int32)


ORDER, CORE = SIDE * SIDE, SIDE * SIDE + SIDE


def turn_kernel(*refs):
    refs[-1][...] = refs[0][...].T


def turn(value, after):
    rows, cols = value.shape
    return pl.pallas_call(
        turn_kernel,
        in_specs=[pl.BlockSpec(memory_space=pltpu.VMEM), pl.BlockSpec(memory_space=pl.ANY)],
        out_specs=pl.BlockSpec(memory_space=pltpu.VMEM),
        out_shape=jax.ShapeDtypeStruct((cols, rows), value.dtype),
        compiler_params=params(8),
        cost_estimate=cost(0, 4 * rows * cols),
        name="turn",
    )(*hbm([value]), after)


def piece_kernel(plan, arrived_count, out_count, extra, carried, blocks, *refs):
    grad_refs, out_refs = refs[:2], refs[2:4]
    arrived_refs = refs[4 : 4 + arrived_count]
    refs = refs[4 + arrived_count + extra :]
    results, refs = refs[:out_count], refs[out_count + carried :]
    if arrived_count:
        outs, grads, held, sent, in_sems, out_sems = refs
    else:
        outs, grads, sent, in_sems, out_sems = refs
    tokens = out_refs[0].shape[1]
    core = blocks[CORE]
    taken = 0

    def load(source, target):
        nonlocal taken
        copy = pltpu.make_async_copy(source, target, in_sems.at[taken])
        taken += 1
        copy.start()
        return copy

    def number(at):
        return blocks[at] if isinstance(at, int) else blocks[blocks[at[0]]]

    shared = [
        load(ref, outs.at[:, n * tokens : (n + 1) * tokens]) for n, ref in enumerate(out_refs)
    ]

    def fetch(n, slot):
        at, parts = plan[n]
        copies = []
        for j, place in enumerate(at):
            first = pl.multiple_of((2 * number(place) + core) * BLK, BLK)
            for k, ref in enumerate(grad_refs):
                copies.append(
                    load(
                        ref.at[:, pl.ds(first, BLK)],
                        grads.at[n, k * tokens : (k + 1) * tokens, j * BLK : (j + 1) * BLK],
                    )
                )
        slots = []
        for _, arrived, _ in parts:
            mine = []
            for which, row, places in arrived:
                rows = arrived_refs[which].at[row : row + WIDE]
                if places is None:
                    copies.append(load(rows, held.at[slot]))
                else:
                    for j, place in enumerate(places):
                        first = pl.multiple_of(blocks[place] * BLK, BLK)
                        copies.append(
                            load(
                                rows.at[:, pl.ds(first, BLK)],
                                held.at[slot, :, j * BLK : (j + 1) * BLK],
                            )
                        )
                mine.append(slot)
                slot += 1
            slots.append(mine)
        return copies, slots, slot

    ahead = fetch(0, 0)
    for copy in shared:
        copy.wait()
    stores, done = [], 0
    for n, (_, parts) in enumerate(plan):
        copies, slots, slot = ahead
        if n + 1 < len(plan):
            ahead = fetch(n + 1, slot)
        for copy in copies:
            copy.wait()
        for (col, _, targets), mine in zip(parts, slots):
            total = jnp.dot(
                outs[col : col + WIDE, :], grads[n], preferred_element_type=jnp.float32
            )
            for k in mine:
                total = total + held[k].astype(jnp.float32)
            sent[done] = total.astype(sent.dtype)
            for out, row, first, count in targets:
                copy = pltpu.make_async_copy(
                    sent.at[done, :, first : first + count],
                    results[out].at[row : row + WIDE],
                    out_sems.at[len(stores)],
                )
                copy.start()
                stores.append(copy)
            done += 1
    for copy in stores:
        copy.wait()


def pieces(name, table, grads, outs, plan, arrived, out_shapes, after=(), carried=()):
    cols, tokens = outs[0].shape
    parts = [part for _, each in plan for part in each]
    terms = [term for part in parts for term in part[1]]
    loads = 2 + 2 * sum(len(at) for at, _ in plan)
    loads += sum(1 if term[2] is None else len(term[2]) for term in terms)
    rows = SIDE * BLK
    scratch = [
        pltpu.VMEM((cols, 2 * tokens), jnp.bfloat16),
        pltpu.VMEM((len(plan), 2 * tokens, rows), jnp.bfloat16),
    ]
    if terms:
        scratch.append(pltpu.VMEM((len(terms), WIDE, rows), jnp.bfloat16))
    scratch += [
        pltpu.VMEM((len(parts), WIDE, rows), jnp.bfloat16),
        pltpu.SemaphoreType.DMA((loads,)),
        pltpu.SemaphoreType.DMA((sum(len(part[2]) for part in parts),)),
    ]
    operands = [*grads, *outs, *arrived, *after]
    at, extra = 1 + len(operands), len(after) + len(carried)
    operands += hbm(carried)
    return pl.pallas_call(
        lambda *refs: piece_kernel(
            plan, len(arrived), len(out_shapes), extra, len(carried), *refs
        ),
        in_specs=[pl.BlockSpec(memory_space=pltpu.SMEM)]
        + [pl.BlockSpec(memory_space=pl.ANY)] * len(operands),
        out_specs=[pl.BlockSpec(memory_space=pl.ANY)] * (len(out_shapes) + len(carried)),
        out_shape=[pltpu.HBM(shape, jnp.bfloat16) for shape in out_shapes]
        + [pltpu.HBM(v.shape, v.dtype) for v in carried],
        input_output_aliases={at + n: len(out_shapes) + n for n in range(len(carried))},
        scratch_shapes=scratch,
        compiler_params=params(PIECES_MIB),
        cost_estimate=cost(
            4 * tokens * rows * WIDE * len(parts),
            2 * (2 * tokens * (cols + len(plan) * rows) + (len(terms) + len(parts)) * rows * WIDE),
        ),
        name=name,
    )(table, *hbm(operands[:1]), *operands[1:])


def chunk(k):
    return [SIDE * k + j for j in range(SIDE)]


def far_stage(table, grads, outs, after):
    rows = SIDE * BLK
    plan = [(chunk(2), [(0, [], [(0, 0, 0, rows)]), (WIDE, [], [(1, 0, 0, rows)])])]
    plus, minus = pieces("far_pieces", table, grads, outs, plan, [], [(WIDE, rows)] * 2, after)
    return [hop(plus, 1), hop(minus, -1)], [plus, minus]


def near_stage(table, grads, outs, after):
    rows = SIDE * BLK
    plan = [
        (chunk(1), [(WIDE, [], [(0, 0, 0, rows)])]),
        (chunk(3), [(0, [], [(1, 0, 0, rows)])]),
    ]
    plus, minus = pieces("near_pieces", table, grads, outs, plan, [], [(WIDE, rows)] * 2, after)
    return [hop(plus, 1), hop(minus, -1)], [plus, minus]


def join_stage(table, grads, outs, far, after):
    rows = SIDE * BLK
    plan = [
        (chunk(1), [(0, [(0, 0, None)], [(0, 0, 0, rows)])]),
        (chunk(3), [(WIDE, [(1, 0, None)], [(1, 0, 0, rows)])]),
    ]
    up, down = pieces("join_pieces", table, grads, outs, plan, far, [(WIDE, rows)] * 2, after)
    return [hop(up, 1), hop(down, -1)], [up, down]


def block_stage(table, grads, outs, near, joined):
    places = [ORDER + n for n in range(SIDE)]
    left = [(n, 0, n * BLK, BLK) for n in range(SIDE)]
    right = [(n, WIDE, n * BLK, BLK) for n in range(SIDE)]
    plan = [
        (
            [(place,) for place in places],
            [
                (0, [(2, 0, places), (1, 0, places)], left),
                (WIDE, [(0, 0, places), (3, 0, places)], right),
            ],
        )
    ]
    two, one, three, mine = pieces(
        "block_pieces",
        table,
        grads,
        outs,
        plan,
        [*near, *joined],
        [(2 * WIDE, BLK)] * SIDE,
    )
    return [mine, hop(two, 2, True), hop(one, 1, True), hop(three, -1, True)]


def total_kernel(*refs):
    total = refs[0][...].astype(jnp.float32)
    for ref in refs[1:-1]:
        total = total + ref[...].astype(jnp.float32)
    refs[-1][...] = total.T


def total_gradient(terms):
    cols, rows = terms[0].shape
    return pl.pallas_call(
        total_kernel,
        in_specs=[pl.BlockSpec(memory_space=pltpu.VMEM)] * len(terms),
        out_specs=pl.BlockSpec(memory_space=pltpu.VMEM),
        out_shape=jax.ShapeDtypeStruct((rows, cols), jnp.float32),
        compiler_params=params(16),
        cost_estimate=cost(4 * rows * cols, 12 * rows * cols),
        name="total_gradient",
    )(*hbm(terms[:1]), *terms[1:])


def attend_kernel(
    low_ref, pos_ref, q_ref, g_ref, o_ref, key_ref, val_ref,
    kv4, kv3, kv2, kv1, after_plus, after_minus,
    packed_ref, own_ref, back4, back32, back1,
    bias, held, keys, keys_t, vals, dkey, dval,
):
    tile = pl.program_id(0)
    scale = 1.0 / math.sqrt(HEAD)
    heads = q_ref.shape[1] // HEAD
    width = heads * TILE
    first = pl.multiple_of(tile * TILE, TILE)

    @pl.when(tile == 0)
    def _():
        for n, ref in enumerate((kv4, kv3, kv2, kv1)):
            keys[n * RUN : (n + 1) * RUN, :] = ref[:, :HEAD]
            vals[n * RUN : (n + 1) * RUN, :] = ref[:, HEAD:]
        keys[BACK * RUN :, :] = key_ref[...]
        vals[BACK * RUN :, :] = val_ref[...]
        keys_t[...] = keys[...].T
        dkey[...] = jnp.zeros_like(dkey)
        dval[...] = jnp.zeros_like(dval)

    row = lax.broadcasted_iota(jnp.int32, (SEEN, TILE), 0)
    col = lax.broadcasted_iota(jnp.int32, (SEEN, TILE), 1)
    low = low_ref[...] - first
    bias[...] = jnp.where((row >= low) & (row <= col + BACK * RUN), 0.0, NEG)

    def stack(ref):
        return jnp.concatenate([ref[:, h * HEAD : (h + 1) * HEAD] for h in range(heads)], axis=0)

    q, g = stack(q_ref), stack(g_ref)
    dots = []
    for h in range(heads):
        part = slice(h * HEAD, (h + 1) * HEAD)
        prod = g_ref[:, part].astype(jnp.float32) * o_ref[:, part].astype(jnp.float32)
        dots.append(jnp.sum(prod.T, axis=0, keepdims=True))
    row_dot = jnp.concatenate(dots, axis=1)
    top = jnp.full((1, width), 2 * NEG, jnp.float32)
    for at in range(0, SEEN, CHUNK):
        rows = pl.ds(pl.multiple_of(first + at, TILE), CHUNK)
        scores = lax.dot_general(keys[rows, :], q, NT, preferred_element_type=jnp.float32)
        mask = jnp.concatenate([bias[at : at + CHUNK, :]] * heads, axis=1)
        scores = scores * (scale * math.log2(math.e)) + mask
        held[at : at + CHUNK, :] = scores
        top = jnp.maximum(top, jnp.max(scores, axis=0, keepdims=True))
    total = jnp.zeros((1, width), jnp.float32)
    for at in range(0, SEEN, CHUNK):
        probs = jnp.exp2(held[at : at + CHUNK, :] - top)
        held[at : at + CHUNK, :] = probs
        total = total + jnp.sum(probs, axis=0, keepdims=True)
    inverse = 1.0 / total
    dq_t = jnp.zeros((HEAD, width), jnp.float32)
    for at in range(0, SEEN, CHUNK):
        rows = pl.ds(pl.multiple_of(first + at, TILE), CHUNK)
        probs = held[at : at + CHUNK, :] * inverse
        dval[rows, :] += jnp.dot(probs.astype(jnp.bfloat16), g, preferred_element_type=jnp.float32)
        prob_grad = lax.dot_general(vals[rows, :], g, NT, preferred_element_type=jnp.float32)
        score_grad = (probs * (prob_grad - row_dot)).astype(jnp.bfloat16)
        dkey[rows, :] += jnp.dot(score_grad, q, preferred_element_type=jnp.float32)
        dq_t += jnp.dot(keys_t[:, rows], score_grad, preferred_element_type=jnp.float32)
    dq_t = dq_t * scale
    dq = jnp.concatenate(
        [dq_t[:, h * TILE : (h + 1) * TILE].T for h in range(heads)], axis=1
    ).astype(jnp.bfloat16)
    slots = lax.broadcasted_iota(jnp.int32, (packed_ref.shape[0], TILE), 0)
    select = (slots == pos_ref[...]).astype(jnp.bfloat16)
    placed = jnp.dot(select, dq, preferred_element_type=jnp.float32).astype(jnp.bfloat16)

    @pl.when(tile == 0)
    def _():
        packed_ref[...] = placed

    @pl.when(tile > 0)
    def _():
        packed_ref[...] += placed

    @pl.when(tile == pl.num_programs(0) - 1)
    def _():
        for n, (ref, at) in enumerate(((back4, 0), (back32, PAIR), (back32, 0), (back1, 0))):
            rows = slice(n * RUN, (n + 1) * RUN)
            ref[:, at : at + HEAD] = (dkey[rows, :] * scale).astype(jnp.bfloat16)
            ref[:, at + HEAD : at + PAIR] = dval[rows, :].astype(jnp.bfloat16)
        own_ref[:, :HEAD] = dkey[BACK * RUN :, :] * scale
        own_ref[:, HEAD:] = dval[BACK * RUN :, :]


def attend(low, pos, query, grad, out, key, value, earlier, slots, after):
    cols = query.shape[1]
    heads = cols // HEAD
    window = (BACK + 1) * RUN
    whole = lambda shape: pl.BlockSpec(shape, lambda t: (0, 0))
    by_tile = pl.BlockSpec((TILE, cols), lambda t: (t, 0))
    pair, double = (RUN, PAIR), (RUN, 2 * PAIR)
    return pl.pallas_call(
        attend_kernel,
        grid=(RUN // TILE,),
        in_specs=[pl.BlockSpec((1, TILE), lambda t: (0, t))] * 2
        + [by_tile] * 3
        + [whole((RUN, HEAD))] * 2
        + [whole(pair)] * BACK
        + [pl.BlockSpec(memory_space=pl.ANY)] * len(after),
        out_specs=[whole((slots, cols)), whole(pair), whole(pair), whole(double), whole(pair)],
        out_shape=[
            pltpu.HBM((slots, cols), jnp.bfloat16),
            pltpu.HBM(pair, jnp.float32),
        ]
        + [pltpu.HBM(shape, jnp.bfloat16) for shape in (pair, double, pair)],
        scratch_shapes=[
            pltpu.VMEM((SEEN, TILE), jnp.float32),
            pltpu.VMEM((SEEN, heads * TILE), jnp.float32),
            pltpu.VMEM((window, HEAD), jnp.bfloat16),
            pltpu.VMEM((HEAD, window), jnp.bfloat16),
            pltpu.VMEM((window, HEAD), jnp.bfloat16),
            pltpu.VMEM((window, HEAD), jnp.float32),
            pltpu.VMEM((window, HEAD), jnp.float32),
        ],
        compiler_params=params(32),
        cost_estimate=cost(10 * heads * RUN * window * HEAD, 8 * MIB, heads * RUN * window),
        name="attend",
    )(*hbm([low, pos, query]), grad, *hbm([out, key, value]), *earlier, *after)


def route_rows(slot_blocks, own_index, parties, block_rows):
    total = slot_blocks.shape[0]
    ids = jnp.arange(total, dtype=jnp.int32)
    slot_of_block = jnp.sum(
        jnp.where(slot_blocks[None, :] == ids[:, None], ids[None, :], 0), axis=1
    )
    local = jnp.arange(parties, dtype=jnp.int32)

    def place(peer, order):
        earlier = (peer[:, None] == peer[None, :]) & (order[None, :] < order[:, None])
        return peer * CAP + jnp.sum(earlier, axis=1).astype(jnp.int32)

    dest_slot = lax.dynamic_slice_in_dim(slot_of_block, own_index * parties, parties, 0)
    held = lax.dynamic_slice_in_dim(slot_blocks, own_index * parties, parties, 0)
    rows = jnp.arange(block_rows, dtype=jnp.int32)

    def spread(at):
        return (at[:, None] * block_rows + rows[None, :]).reshape(-1)

    return spread(place(dest_slot // parties, dest_slot)), spread(place(held // parties, local))


def on_device(
    grad_out, out_weight, query_states, key_states, value_tensor, attn_out, doc_ids, block_order
):
    parties = lax.axis_size("ctx")
    own_index = lax.axis_index("ctx")
    core = lax.axis_index("dp")
    x, y = own_index // SIDE, own_index % SIDE
    grad_rows, out_rows = grad_out[0], attn_out[0]
    doc_row = doc_ids[0]
    key, value = key_states[0], value_tensor[0]

    both = jnp.concatenate([key, value], axis=1)
    earlier = [lax.ppermute(both, "ctx", run_shift(k, parties)) for k in range(BACK, 0, -1)]

    table = block_table(x, y, core)
    grads = [grad_rows, swap_cores(grad_rows)]
    turned = turn(out_rows, grads[1])
    outs = [turned, swap_cores(turned)]
    far, far_sent = far_stage(table, grads, outs, earlier)
    near, near_sent = near_stage(table, grads, outs, hbm(far_sent))
    attn_grad = project(grad_rows, out_weight, *hbm(near_sent[:1]))
    joined, joined_sent = join_stage(table, grads, outs, far, [attn_grad])
    own_docs = lax.dynamic_slice_in_dim(doc_row, own_index * RUN, RUN, 0)
    start = jnp.maximum(own_index - BACK, 0) * RUN
    seen_docs = lax.dynamic_slice_in_dim(doc_row, start, (BACK + 1) * RUN, 0)
    first = start + jnp.sum((seen_docs[:, None] < own_docs[None, :]).astype(jnp.int32), axis=0)
    low = (first - (own_index - BACK) * RUN).reshape(1, RUN)
    send_rows, held_rows = route_rows(block_order[0], own_index, parties, RUN // parties)
    slots = CAP * RUN
    packed, own_kv, back4, back32, back1 = attend(
        low,
        send_rows.reshape(1, RUN),
        query_states[0],
        attn_grad,
        out_rows,
        key,
        value,
        earlier,
        slots,
        hbm(joined_sent),
    )
    got = lax.all_to_all(
        packed.reshape(parties, slots // parties, -1), "ctx", 0, 0, tiled=True
    ).reshape(slots, -1)
    held_select = (
        held_rows[:, None] == jnp.arange(slots, dtype=jnp.int32)[None, :]
    ).astype(jnp.bfloat16)
    query_grad = jnp.dot(held_select, got, preferred_element_type=jnp.float32).astype(jnp.bfloat16)
    terms = block_stage(table, grads, outs, near, joined)
    back32 = lax.ppermute(back32, "ctx", run_shift(-2, parties))
    back4 = lax.ppermute(back4, "ctx", run_shift(-4, parties))
    joint = back1.astype(jnp.float32) + back32[:, PAIR:].astype(jnp.float32)
    back1 = lax.ppermute(joint.astype(jnp.bfloat16), "ctx", run_shift(-1, parties))
    returned = [back32[:, :PAIR], back4, back1]
    kv_sum = own_kv
    for v in returned:
        kv_sum = kv_sum + v.astype(jnp.float32)
    kv_sum = kv_sum.astype(jnp.bfloat16)
    weight_grad = total_gradient(terms)
    return (
        query_grad[None],
        kv_sum[None, :, :HEAD],
        kv_sum[None, :, HEAD:],
        weight_grad,
    )


def solution(mesh):
    heads = P("dp", "ctx", "tp")
    in_specs = (
        P("dp", "ctx", None),
        P(None, "tp"),
        heads,
        heads,
        heads,
        heads,
        P("dp", None),
        P("dp", None),
    )
    out_specs = (heads, heads, heads, P(("ctx", "dp"), "tp"))
    return jax.shard_map(
        on_device, mesh=mesh, in_specs=in_specs, out_specs=out_specs, check_vma=False
    )
```

```python
import math

import jax
import jax.numpy as jnp
from jax import lax
from jax.experimental import pallas as pl
from jax.experimental.pallas import tpu as pltpu
from jax.sharding import PartitionSpec as P

HEAD = 128
CAP = 2
SIDE = 4
BACK = 4
RUN = 256
BLK = 256
TILE = 128
SEEN = BACK * RUN + TILE
CHUNK = 1152
PIECES_MIB = 24
WIDE = 512
PAIR = 2 * HEAD
NEG = -1e30
MIB = 1024 * 1024
NT = (((1,), (1,)), ((), ()))
TN = (((0,), (0,)), ((), ()))


def run_shift(k, parties):
    return [(i, (i + k) % parties) for i in range(parties)]


def axis_shift(k, second):
    pairs = []
    for x in range(SIDE):
        for y in range(SIDE):
            for core in range(2):
                along_x = (core == 0) != second
                to_x, to_y = ((x + k) % SIDE, y) if along_x else (x, (y + k) % SIDE)
                pairs.append(((x * SIDE + y) * 2 + core, (to_x * SIDE + to_y) * 2 + core))
    return pairs


def hop(value, k, second=False):
    return lax.ppermute(value, ("ctx", "dp"), axis_shift(k, second))


def swap_cores(value):
    return lax.ppermute(value, "dp", [(0, 1), (1, 0)])


def params(mib):
    return pltpu.CompilerParams(vmem_limit_bytes=mib * MIB)


def hbm(values):
    return [pltpu.with_memory_space_constraint(v, pltpu.HBM) for v in values]


def cost(flops, moved, exps=0):
    return pl.CostEstimate(flops=flops, bytes_accessed=moved, transcendentals=exps)


def project_kernel(grad_ref, weight_ref, after_ref, out_ref, grads, weights, grad_sems, weight_sems):
    slabs = grad_sems.shape[0]
    depth = weight_ref.shape[0] // slabs
    copies = []
    for i in range(slabs):
        part = slice(i * depth, (i + 1) * depth)
        copies.append(
            (
                pltpu.make_async_copy(grad_ref.at[:, part], grads.at[:, part], grad_sems.at[i]),
                pltpu.make_async_copy(weight_ref.at[part], weights.at[part], weight_sems.at[i]),
            )
        )
    for pair in copies:
        for copy in pair:
            copy.start()
    total = None
    for i, pair in enumerate(copies):
        for copy in pair:
            copy.wait()
        part = slice(i * depth, (i + 1) * depth)
        addend = jnp.dot(grads[:, part], weights[part, :], preferred_element_type=jnp.float32)
        total = addend if total is None else total + addend
    out_ref[...] = total.astype(out_ref.dtype)


def project(grad_rows, weight, after):
    rows, depth = grad_rows.shape
    cols = weight.shape[1]
    slabs = 8
    return pl.pallas_call(
        project_kernel,
        in_specs=[pl.BlockSpec(memory_space=pl.ANY)] * 3,
        out_specs=pl.BlockSpec(memory_space=pltpu.VMEM),
        out_shape=jax.ShapeDtypeStruct((rows, cols), jnp.bfloat16),
        scratch_shapes=[
            pltpu.VMEM(grad_rows.shape, grad_rows.dtype),
            pltpu.VMEM(weight.shape, weight.dtype),
            pltpu.SemaphoreType.DMA((slabs,)),
            pltpu.SemaphoreType.DMA((slabs,)),
        ],
        compiler_params=params(32),
        cost_estimate=cost(2 * rows * depth * cols, 2 * depth * (rows + cols)),
        name="project",
    )(*hbm([grad_rows, weight]), after)


def block_table(x, y, core):
    first, second = jnp.where(core == 0, x, y), jnp.where(core == 0, y, x)
    step_first, step_second = jnp.where(core == 0, SIDE, 1), jnp.where(core == 0, 1, SIDE)
    offsets = jnp.arange(SIDE, dtype=jnp.int32)
    blocks = ((first + offsets[:, None]) % SIDE) * step_first + offsets[None, :] * step_second
    order = (second + jnp.stack([jnp.int32(v) for v in (2, 1, 3, 0)])) % SIDE
    table = jnp.concatenate([blocks.reshape(-1), order, core.reshape(1)])
    return table.astype(jnp.int32)


ORDER, CORE = SIDE * SIDE, SIDE * SIDE + SIDE


def turn_kernel(*refs):
    refs[-1][...] = refs[0][...].T


def turn(value, after):
    rows, cols = value.shape
    return pl.pallas_call(
        turn_kernel,
        in_specs=[pl.BlockSpec(memory_space=pltpu.VMEM), pl.BlockSpec(memory_space=pl.ANY)],
        out_specs=pl.BlockSpec(memory_space=pltpu.VMEM),
        out_shape=jax.ShapeDtypeStruct((cols, rows), value.dtype),
        compiler_params=params(8),
        cost_estimate=cost(0, 4 * rows * cols),
        name="turn",
    )(*hbm([value]), after)


def piece_kernel(plan, arrived_count, out_count, extra, carried, blocks, *refs):
    grad_refs, out_refs = refs[:2], refs[2:4]
    arrived_refs = refs[4 : 4 + arrived_count]
    refs = refs[4 + arrived_count + extra :]
    results, refs = refs[:out_count], refs[out_count + carried :]
    if arrived_count:
        outs, grads, held, sent, in_sems, out_sems = refs
    else:
        outs, grads, sent, in_sems, out_sems = refs
    tokens = out_refs[0].shape[1]
    core = blocks[CORE]
    taken = 0

    def load(source, target):
        nonlocal taken
        copy = pltpu.make_async_copy(source, target, in_sems.at[taken])
        taken += 1
        copy.start()
        return copy

    def number(at):
        return blocks[at] if isinstance(at, int) else blocks[blocks[at[0]]]

    shared = [
        load(ref, outs.at[:, n * tokens : (n + 1) * tokens]) for n, ref in enumerate(out_refs)
    ]

    def fetch(n, slot):
        at, parts = plan[n]
        copies = []
        for j, place in enumerate(at):
            first = pl.multiple_of((2 * number(place) + core) * BLK, BLK)
            for k, ref in enumerate(grad_refs):
                copies.append(
                    load(
                        ref.at[:, pl.ds(first, BLK)],
                        grads.at[n, k * tokens : (k + 1) * tokens, j * BLK : (j + 1) * BLK],
                    )
                )
        slots = []
        for _, arrived, _ in parts:
            mine = []
            for which, row, places in arrived:
                rows = arrived_refs[which].at[row : row + WIDE]
                if places is None:
                    copies.append(load(rows, held.at[slot]))
                else:
                    for j, place in enumerate(places):
                        first = pl.multiple_of(blocks[place] * BLK, BLK)
                        copies.append(
                            load(
                                rows.at[:, pl.ds(first, BLK)],
                                held.at[slot, :, j * BLK : (j + 1) * BLK],
                            )
                        )
                mine.append(slot)
                slot += 1
            slots.append(mine)
        return copies, slots, slot

    ahead = fetch(0, 0)
    for copy in shared:
        copy.wait()
    stores, done = [], 0
    for n, (_, parts) in enumerate(plan):
        copies, slots, slot = ahead
        if n + 1 < len(plan):
            ahead = fetch(n + 1, slot)
        for copy in copies:
            copy.wait()
        for (col, _, targets), mine in zip(parts, slots):
            total = jnp.dot(
                outs[col : col + WIDE, :], grads[n], preferred_element_type=jnp.float32
            )
            for k in mine:
                total = total + held[k].astype(jnp.float32)
            sent[done] = total.astype(sent.dtype)
            for out, row, first, count in targets:
                copy = pltpu.make_async_copy(
                    sent.at[done, :, first : first + count],
                    results[out].at[row : row + WIDE],
                    out_sems.at[len(stores)],
                )
                copy.start()
                stores.append(copy)
            done += 1
    for copy in stores:
        copy.wait()


def pieces(name, table, grads, outs, plan, arrived, out_shapes, after=(), carried=()):
    cols, tokens = outs[0].shape
    parts = [part for _, each in plan for part in each]
    terms = [term for part in parts for term in part[1]]
    loads = 2 + 2 * sum(len(at) for at, _ in plan)
    loads += sum(1 if term[2] is None else len(term[2]) for term in terms)
    rows = SIDE * BLK
    scratch = [
        pltpu.VMEM((cols, 2 * tokens), jnp.bfloat16),
        pltpu.VMEM((len(plan), 2 * tokens, rows), jnp.bfloat16),
    ]
    if terms:
        scratch.append(pltpu.VMEM((len(terms), WIDE, rows), jnp.bfloat16))
    scratch += [
        pltpu.VMEM((len(parts), WIDE, rows), jnp.bfloat16),
        pltpu.SemaphoreType.DMA((loads,)),
        pltpu.SemaphoreType.DMA((sum(len(part[2]) for part in parts),)),
    ]
    operands = [*grads, *outs, *arrived, *after]
    at, extra = 1 + len(operands), len(after) + len(carried)
    operands += hbm(carried)
    return pl.pallas_call(
        lambda *refs: piece_kernel(
            plan, len(arrived), len(out_shapes), extra, len(carried), *refs
        ),
        in_specs=[pl.BlockSpec(memory_space=pltpu.SMEM)]
        + [pl.BlockSpec(memory_space=pl.ANY)] * len(operands),
        out_specs=[pl.BlockSpec(memory_space=pl.ANY)] * (len(out_shapes) + len(carried)),
        out_shape=[pltpu.HBM(shape, jnp.bfloat16) for shape in out_shapes]
        + [pltpu.HBM(v.shape, v.dtype) for v in carried],
        input_output_aliases={at + n: len(out_shapes) + n for n in range(len(carried))},
        scratch_shapes=scratch,
        compiler_params=params(PIECES_MIB),
        cost_estimate=cost(
            4 * tokens * rows * WIDE * len(parts),
            2 * (2 * tokens * (cols + len(plan) * rows) + (len(terms) + len(parts)) * rows * WIDE),
        ),
        name=name,
    )(table, *hbm(operands[:1]), *operands[1:])


def chunk(k):
    return [SIDE * k + j for j in range(SIDE)]


def far_stage(table, grads, outs, after):
    rows = SIDE * BLK
    plan = [(chunk(2), [(0, [], [(0, 0, 0, rows)]), (WIDE, [], [(1, 0, 0, rows)])])]
    plus, minus = pieces("far_pieces", table, grads, outs, plan, [], [(WIDE, rows)] * 2, after)
    return [hop(plus, 1), hop(minus, -1)], [plus, minus]


def near_stage(table, grads, outs, after):
    rows = SIDE * BLK
    plan = [
        (chunk(1), [(WIDE, [], [(0, 0, 0, rows)])]),
        (chunk(3), [(0, [], [(1, 0, 0, rows)])]),
    ]
    plus, minus = pieces("near_pieces", table, grads, outs, plan, [], [(WIDE, rows)] * 2, after)
    return [hop(plus, 1), hop(minus, -1)], [plus, minus]


def join_stage(table, grads, outs, far, after):
    rows = SIDE * BLK
    plan = [
        (chunk(1), [(0, [(0, 0, None)], [(0, 0, 0, rows)])]),
        (chunk(3), [(WIDE, [(1, 0, None)], [(1, 0, 0, rows)])]),
    ]
    up, down = pieces("join_pieces", table, grads, outs, plan, far, [(WIDE, rows)] * 2, after)
    return [hop(up, 1), hop(down, -1)], [up, down]


def block_stage(table, grads, outs, near, joined):
    places = [ORDER + n for n in range(SIDE)]
    left = [(n, 0, n * BLK, BLK) for n in range(SIDE)]
    right = [(n, WIDE, n * BLK, BLK) for n in range(SIDE)]
    plan = [
        (
            [(place,) for place in places],
            [
                (0, [(2, 0, places), (1, 0, places)], left),
                (WIDE, [(0, 0, places), (3, 0, places)], right),
            ],
        )
    ]
    two, one, three, mine = pieces(
        "block_pieces",
        table,
        grads,
        outs,
        plan,
        [*near, *joined],
        [(2 * WIDE, BLK)] * SIDE,
    )
    return [mine, hop(two, 2, True), hop(one, 1, True), hop(three, -1, True)]


def partial_kernel(*refs):
    total = refs[0][...].astype(jnp.float32)
    for ref in refs[1:-1]:
        total = total + ref[...].astype(jnp.float32)
    refs[-1][...] = total.T


def total_kernel(partial_ref, last_ref, out_ref):
    out_ref[...] = partial_ref[...] + last_ref[...].astype(jnp.float32).T


def summed(kernel, name, operands, shape):
    return pl.pallas_call(
        kernel,
        in_specs=[pl.BlockSpec(memory_space=pltpu.VMEM)] * len(operands),
        out_specs=pl.BlockSpec(memory_space=pltpu.VMEM),
        out_shape=jax.ShapeDtypeStruct(shape, jnp.float32),
        compiler_params=params(16),
        cost_estimate=cost(4 * shape[0] * shape[1], 12 * shape[0] * shape[1]),
        name=name,
    )(*operands)


def total_gradient(terms):
    mine, two, one, three = terms
    shape = mine.shape[::-1]
    partial = summed(partial_kernel, "partial_gradient", [*hbm([mine]), two, three], shape)
    return summed(total_kernel, "total_gradient", [partial, one], shape)


def attend_kernel(
    low_ref, pos_ref, q_ref, g_ref, o_ref, key_ref, val_ref,
    kv4, kv3, kv2, kv1, after_plus, after_minus,
    packed_ref, own_ref, back4, back32, back1,
    bias, held, keys, keys_t, vals, dkey, dval,
):
    tile = pl.program_id(0)
    scale = 1.0 / math.sqrt(HEAD)
    heads = q_ref.shape[1] // HEAD
    width = heads * TILE
    first = pl.multiple_of(tile * TILE, TILE)

    @pl.when(tile == 0)
    def _():
        for n, ref in enumerate((kv4, kv3, kv2, kv1)):
            keys[n * RUN : (n + 1) * RUN, :] = ref[:, :HEAD]
            vals[n * RUN : (n + 1) * RUN, :] = ref[:, HEAD:]
        keys[BACK * RUN :, :] = key_ref[...]
        vals[BACK * RUN :, :] = val_ref[...]
        keys_t[...] = keys[...].T
        dkey[...] = jnp.zeros_like(dkey)
        dval[...] = jnp.zeros_like(dval)

    row = lax.broadcasted_iota(jnp.int32, (SEEN, TILE), 0)
    col = lax.broadcasted_iota(jnp.int32, (SEEN, TILE), 1)
    low = low_ref[...] - first
    bias[...] = jnp.where((row >= low) & (row <= col + BACK * RUN), 0.0, NEG)

    def stack(ref):
        return jnp.concatenate([ref[:, h * HEAD : (h + 1) * HEAD] for h in range(heads)], axis=0)

    q, g = stack(q_ref), stack(g_ref)
    dots = []
    for h in range(heads):
        part = slice(h * HEAD, (h + 1) * HEAD)
        prod = g_ref[:, part].astype(jnp.float32) * o_ref[:, part].astype(jnp.float32)
        dots.append(jnp.sum(prod.T, axis=0, keepdims=True))
    row_dot = jnp.concatenate(dots, axis=1)
    top = jnp.full((1, width), 2 * NEG, jnp.float32)
    for at in range(0, SEEN, CHUNK):
        rows = pl.ds(pl.multiple_of(first + at, TILE), CHUNK)
        scores = lax.dot_general(keys[rows, :], q, NT, preferred_element_type=jnp.float32)
        mask = jnp.concatenate([bias[at : at + CHUNK, :]] * heads, axis=1)
        scores = scores * (scale * math.log2(math.e)) + mask
        held[at : at + CHUNK, :] = scores
        top = jnp.maximum(top, jnp.max(scores, axis=0, keepdims=True))
    total = jnp.zeros((1, width), jnp.float32)
    for at in range(0, SEEN, CHUNK):
        probs = jnp.exp2(held[at : at + CHUNK, :] - top)
        held[at : at + CHUNK, :] = probs
        total = total + jnp.sum(probs, axis=0, keepdims=True)
    inverse = 1.0 / total
    dq_t = jnp.zeros((HEAD, width), jnp.float32)
    for at in range(0, SEEN, CHUNK):
        rows = pl.ds(pl.multiple_of(first + at, TILE), CHUNK)
        probs = held[at : at + CHUNK, :] * inverse
        dval[rows, :] += jnp.dot(probs.astype(jnp.bfloat16), g, preferred_element_type=jnp.float32)
        prob_grad = lax.dot_general(vals[rows, :], g, NT, preferred_element_type=jnp.float32)
        score_grad = (probs * (prob_grad - row_dot)).astype(jnp.bfloat16)
        dkey[rows, :] += jnp.dot(score_grad, q, preferred_element_type=jnp.float32)
        dq_t += jnp.dot(keys_t[:, rows], score_grad, preferred_element_type=jnp.float32)
    dq_t = dq_t * scale
    dq = jnp.concatenate(
        [dq_t[:, h * TILE : (h + 1) * TILE].T for h in range(heads)], axis=1
    ).astype(jnp.bfloat16)
    slots = lax.broadcasted_iota(jnp.int32, (packed_ref.shape[0], TILE), 0)
    select = (slots == pos_ref[...]).astype(jnp.bfloat16)
    placed = jnp.dot(select, dq, preferred_element_type=jnp.float32).astype(jnp.bfloat16)

    @pl.when(tile == 0)
    def _():
        packed_ref[...] = placed

    @pl.when(tile > 0)
    def _():
        packed_ref[...] += placed

    @pl.when(tile == pl.num_programs(0) - 1)
    def _():
        for n, (ref, at) in enumerate(((back4, 0), (back32, PAIR), (back32, 0), (back1, 0))):
            rows = slice(n * RUN, (n + 1) * RUN)
            ref[:, at : at + HEAD] = (dkey[rows, :] * scale).astype(jnp.bfloat16)
            ref[:, at + HEAD : at + PAIR] = dval[rows, :].astype(jnp.bfloat16)
        own_ref[:, :HEAD] = dkey[BACK * RUN :, :] * scale
        own_ref[:, HEAD:] = dval[BACK * RUN :, :]


def attend(low, pos, query, grad, out, key, value, earlier, slots, after):
    cols = query.shape[1]
    heads = cols // HEAD
    window = (BACK + 1) * RUN
    whole = lambda shape: pl.BlockSpec(shape, lambda t: (0, 0))
    by_tile = pl.BlockSpec((TILE, cols), lambda t: (t, 0))
    pair, double = (RUN, PAIR), (RUN, 2 * PAIR)
    return pl.pallas_call(
        attend_kernel,
        grid=(RUN // TILE,),
        in_specs=[pl.BlockSpec((1, TILE), lambda t: (0, t))] * 2
        + [by_tile] * 3
        + [whole((RUN, HEAD))] * 2
        + [whole(pair)] * BACK
        + [pl.BlockSpec(memory_space=pl.ANY)] * len(after),
        out_specs=[whole((slots, cols)), whole(pair), whole(pair), whole(double), whole(pair)],
        out_shape=[
            pltpu.HBM((slots, cols), jnp.bfloat16),
            pltpu.HBM(pair, jnp.float32),
        ]
        + [pltpu.HBM(shape, jnp.bfloat16) for shape in (pair, double, pair)],
        scratch_shapes=[
            pltpu.VMEM((SEEN, TILE), jnp.float32),
            pltpu.VMEM((SEEN, heads * TILE), jnp.float32),
            pltpu.VMEM((window, HEAD), jnp.bfloat16),
            pltpu.VMEM((HEAD, window), jnp.bfloat16),
            pltpu.VMEM((window, HEAD), jnp.bfloat16),
            pltpu.VMEM((window, HEAD), jnp.float32),
            pltpu.VMEM((window, HEAD), jnp.float32),
        ],
        compiler_params=params(32),
        cost_estimate=cost(10 * heads * RUN * window * HEAD, 8 * MIB, heads * RUN * window),
        name="attend",
    )(*hbm([low, pos, query]), grad, *hbm([out, key, value]), *earlier, *after)


def route_rows(slot_blocks, own_index, parties, block_rows):
    total = slot_blocks.shape[0]
    ids = jnp.arange(total, dtype=jnp.int32)
    slot_of_block = jnp.sum(
        jnp.where(slot_blocks[None, :] == ids[:, None], ids[None, :], 0), axis=1
    )
    local = jnp.arange(parties, dtype=jnp.int32)

    def place(peer, order):
        earlier = (peer[:, None] == peer[None, :]) & (order[None, :] < order[:, None])
        return peer * CAP + jnp.sum(earlier, axis=1).astype(jnp.int32)

    dest_slot = lax.dynamic_slice_in_dim(slot_of_block, own_index * parties, parties, 0)
    held = lax.dynamic_slice_in_dim(slot_blocks, own_index * parties, parties, 0)
    rows = jnp.arange(block_rows, dtype=jnp.int32)

    def spread(at):
        return (at[:, None] * block_rows + rows[None, :]).reshape(-1)

    return spread(place(dest_slot // parties, dest_slot)), spread(place(held // parties, local))


def on_device(
    grad_out, out_weight, query_states, key_states, value_tensor, attn_out, doc_ids, block_order
):
    parties = lax.axis_size("ctx")
    own_index = lax.axis_index("ctx")
    core = lax.axis_index("dp")
    x, y = own_index // SIDE, own_index % SIDE
    grad_rows, out_rows = grad_out[0], attn_out[0]
    doc_row = doc_ids[0]
    key, value = key_states[0], value_tensor[0]

    both = jnp.concatenate([key, value], axis=1)
    earlier = [lax.ppermute(both, "ctx", run_shift(k, parties)) for k in range(BACK, 0, -1)]

    table = block_table(x, y, core)
    grads = [grad_rows, swap_cores(grad_rows)]
    turned = turn(out_rows, grads[1])
    outs = [turned, swap_cores(turned)]
    far, far_sent = far_stage(table, grads, outs, earlier)
    near, near_sent = near_stage(table, grads, outs, hbm(far_sent))
    attn_grad = project(grad_rows, out_weight, *hbm(near_sent[:1]))
    joined, joined_sent = join_stage(table, grads, outs, far, [attn_grad])
    own_docs = lax.dynamic_slice_in_dim(doc_row, own_index * RUN, RUN, 0)
    start = jnp.maximum(own_index - BACK, 0) * RUN
    seen_docs = lax.dynamic_slice_in_dim(doc_row, start, (BACK + 1) * RUN, 0)
    first = start + jnp.sum((seen_docs[:, None] < own_docs[None, :]).astype(jnp.int32), axis=0)
    low = (first - (own_index - BACK) * RUN).reshape(1, RUN)
    send_rows, held_rows = route_rows(block_order[0], own_index, parties, RUN // parties)
    slots = CAP * RUN
    packed, own_kv, back4, back32, back1 = attend(
        low,
        send_rows.reshape(1, RUN),
        query_states[0],
        attn_grad,
        out_rows,
        key,
        value,
        earlier,
        slots,
        hbm(joined_sent),
    )
    got = lax.all_to_all(
        packed.reshape(parties, slots // parties, -1), "ctx", 0, 0, tiled=True
    ).reshape(slots, -1)
    held_select = (
        held_rows[:, None] == jnp.arange(slots, dtype=jnp.int32)[None, :]
    ).astype(jnp.bfloat16)
    query_grad = jnp.dot(held_select, got, preferred_element_type=jnp.float32).astype(jnp.bfloat16)
    terms = block_stage(table, grads, outs, near, joined)
    back32 = lax.ppermute(back32, "ctx", run_shift(-2, parties))
    back4 = lax.ppermute(back4, "ctx", run_shift(-4, parties))
    joint = back1.astype(jnp.float32) + back32[:, PAIR:].astype(jnp.float32)
    back1 = lax.ppermute(joint.astype(jnp.bfloat16), "ctx", run_shift(-1, parties))
    returned = [back32[:, :PAIR], back4, back1]
    kv_sum = own_kv
    for v in returned:
        kv_sum = kv_sum + v.astype(jnp.float32)
    kv_sum = kv_sum.astype(jnp.bfloat16)
    weight_grad = total_gradient(terms)
    return (
        query_grad[None],
        kv_sum[None, :, :HEAD],
        kv_sum[None, :, HEAD:],
        weight_grad,
    )


def solution(mesh):
    heads = P("dp", "ctx", "tp")
    in_specs = (
        P("dp", "ctx", None),
        P(None, "tp"),
        heads,
        heads,
        heads,
        heads,
        P("dp", None),
        P("dp", None),
    )
    out_specs = (heads, heads, heads, P(("ctx", "dp"), "tp"))
    return jax.shard_map(
        on_device, mesh=mesh, in_specs=in_specs, out_specs=out_specs, check_vma=False
    )
```
